256 devices in a mesh: ctx: 8 (over y, core), exp: 32 (over z, x).
Axes of the slice: x: 4, y: 4, z: 8, core: 2. Of those that a mesh axis runs over, the one named last changes fastest.
Arguments:
- kv_cache: bfloat16 [32, 192, 2, 32, 512], P('exp', 'ctx'), may hold values from -6 to 30
- slot_owner: int32 [32, 192], P('exp', 'ctx'), may hold values from -1 to 3, as said below
- slot_fill: int32 [32, 192], P('exp', 'ctx'), may hold values from 1 to 32
- phased: bfloat16 [32, 64, 2, 32, 512], P('exp', 'ctx'), may hold values from -6 to 30
- phase_owner: int32 [32, 64], P('exp'), may hold values from 0 to 3
- phase_fill: int32 [32, 64], P('exp'), may hold values from 1 to 32
- relay_page: int32 [32, 8, 8], P('exp'), may hold values from -1 to 7, as said below
- relay_slot: int32 [32, 8, 8], P('exp'), may hold values from 0 to 23, as said below
- queries: bfloat16 [2, 128, 6, 8192], P(None, 'exp'), may hold values from -6 to 120
- new_kv: bfloat16 [2, 128, 6, 2, 512], P(None, 'exp'), may hold values from -6 to 30
- hidden_in: bfloat16 [2, 128, 6, 4096], P(None, 'exp'), may hold values from -18 to 18
- o_proj: bfloat16 [8192, 4096], P('ctx', 'exp'), may hold values from -0.5 to 0.5
- expert_ids: int32 [2, 128, 6, 8], P(None, 'exp'), may hold values from 0 to 63, all different within a row; in each aligned block of 24 rows (0 to 23, 24 to 47, ..., all dimensions but the last counted through in order) at most 6 rows name the same one
- gate_weights: float32 [2, 128, 6, 8], P(None, 'exp'), may hold values from 0.05 to 1
- w_gate: bfloat16 [64, 4096, 1536], P('exp', None, 'ctx'), may hold values from -0.09375 to 0.09375
- w_up: bfloat16 [64, 4096, 1536], P('exp', None, 'ctx'), may hold values from -0.09375 to 0.09375
- w_down: bfloat16 [64, 1536, 4096], P('exp', 'ctx'), may hold values from -0.15625 to 0.15625
Outputs:
- layer_out: bfloat16 [2, 128, 6, 4096], P(None, 'exp', None, 'ctx')
The draws below stay inside these ranges and needn't reach their ends.
Inputs may be any that keep to these rules, and one draw needn't show every extreme that they name: `slot_owner`: local index within the group's 4 requests of the page a slot holds, -1 for an empty slot; every device holds at least 8 empty slots, and one device of each group exactly 8. `relay_page`: index within the source's 8 phased pages of the page that source s of a group sends to destination d, or -1; a source names each phased page at most once; in every group some destination receives a page from every source. `relay_slot`: slot of destination d receiving that page; the slots named for one destination are distinct and empty in slot_owner. `expert_ids`: in the 24 rows of one index of exp and one step (aligned blocks), no expert is named more than 6 times.
All inputs are finite; a program needn't handle non-finite values.
Results may differ from the reference program's by a relative error of at most 0.02.
Values may be sent and summed in bfloat16 or wider, within the bound.
No kernel may reach another device: no remote copies, remote signals or barrier semaphores. Data moves between devices by JAX's collectives and lax.ppermute only.
A program may use at most 128 MiB of HBM per device.

```python
import math
import jax
import jax.numpy as jnp
import numpy as np
from jax import lax

D = 4096
HEADS = 64
KV_HEADS = 4
HEAD = 128
FF = 1536
TOPK = 8
REQ_DEV = 4
DRAFT = 6
STEPS = 2
PAGE = 32
SLOTS = 24
SECTION = 8
EXPERTS = 64
GROUPS = 32
REQS = 128
CTX_SLOTS = 192
CTX_SECTION = 64
QW = 8192
CAP = 6
N_CTX = 8
N_EXP = 32


def lifted_keys(key, lead, middle, lift):
    normal_key = jax.random.fold_in(key, 0)
    shape = lead + (2,) + middle + (KV_HEADS, HEAD)
    sample = jnp.clip(jax.random.normal(normal_key, shape, jnp.float32), -6.0, 6.0)
    first_kind = (jnp.arange(2) == 0).astype(jnp.float32).reshape((2,) + (1,) * (len(middle) + 2))
    first_entry = (jnp.arange(HEAD) == 0).astype(jnp.float32)
    chosen = lift * first_kind * first_entry
    sample = sample * (1.0 - chosen)
    return sample.reshape(lead + (2,) + middle + (KV_HEADS * HEAD,))


def slot_layout(key):
    order_key, count_key, hub_key = jax.random.split(key, 3)
    device_keys = jax.random.split(order_key, GROUPS * N_CTX)
    slot_order = jax.vmap(lambda one_key: jax.random.permutation(one_key, SLOTS))(device_keys).reshape(GROUPS, N_CTX, SLOTS)
    used_count = jax.random.randint(count_key, (GROUPS, N_CTX), 1, SLOTS - N_CTX + 1)
    hub_device = jax.random.randint(hub_key, (GROUPS, 1), 0, N_CTX)
    used_count = jnp.where(jnp.arange(N_CTX)[None, :] == hub_device, SLOTS - N_CTX, used_count)
    return (slot_order, used_count)


def draw_kv_cache(key, part):
    key = jax.random.fold_in(key, 1)
    lift = 0.0
    return lifted_keys(key, (GROUPS, CTX_SLOTS), (PAGE,), lift).astype(jnp.bfloat16)


def draw_phased(key, part):
    key = jax.random.fold_in(key, 2)
    lift = 0.0
    return lifted_keys(key, (GROUPS, CTX_SECTION), (PAGE,), lift).astype(jnp.bfloat16)


def draw_new_kv(key, part):
    key = jax.random.fold_in(key, 3)
    lift = 0.0
    return lifted_keys(key, (STEPS, REQS, DRAFT), (), lift).astype(jnp.bfloat16)


def draw_queries(key, part):
    key = jax.random.fold_in(key, 4)
    normal_key, pick_key = jax.random.split(key, 2)
    shape = (STEPS, REQS, DRAFT, HEADS, HEAD)
    sample = jnp.clip(jax.random.normal(normal_key, shape, jnp.float32), -6.0, 6.0)
    lift = 0.0
    picked = (jax.random.randint(pick_key, (STEPS, REQS, DRAFT, HEADS, 1), 0, 4) == 0).astype(jnp.float32)
    first_entry = (jnp.arange(HEAD) == 0).astype(jnp.float32)
    chosen = lift * picked * first_entry
    sample = sample * (1.0 - chosen)
    return sample.reshape(STEPS, REQS, DRAFT, HEADS * HEAD).astype(jnp.bfloat16)


def draw_hidden_in(key, part):
    key = jax.random.fold_in(key, 5)
    normal_key, row_key, column_key = jax.random.split(key, 3)
    shape = (STEPS, REQS, DRAFT, D)
    sample = jnp.clip(jax.random.normal(normal_key, shape, jnp.float32), -6.0, 6.0)
    row_scale = jnp.exp(jax.random.uniform(row_key, (STEPS, REQS, DRAFT, 1), jnp.float32, jnp.log(0.1), 0.0))
    column_scale = jnp.exp(jax.random.uniform(column_key, (D,), jnp.float32, jnp.log(0.3), jnp.log(3.0)))
    return (sample * row_scale * column_scale).astype(jnp.bfloat16)


def draw_slot_owner(key, part):
    slot_order, used_count = slot_layout(key)
    key = jax.random.fold_in(key, 6)
    position = jnp.argsort(slot_order, axis=-1)
    request = jax.random.randint(key, (GROUPS, N_CTX, SLOTS), 0, REQ_DEV)
    owners = jnp.where(position < used_count[..., None], request, -1)
    return owners.reshape(GROUPS, N_CTX * SLOTS).astype(jnp.int32)


def draw_relay_slot(key, part):
    slot_order, used_count = slot_layout(key)
    offset = used_count[:, None, :] + jnp.arange(N_CTX)[None, :, None]
    table = jnp.broadcast_to(slot_order[:, None], (GROUPS, N_CTX, N_CTX, SLOTS))
    return jnp.take_along_axis(table, offset[..., None], axis=3)[..., 0].astype(jnp.int32)


def draw_relay_page(key, part):
    key = jax.random.fold_in(key, 8)
    perm_key, coin_key, hub_key = jax.random.split(key, 3)
    source_keys = jax.random.split(perm_key, GROUPS * N_CTX)
    phase_perm = jax.vmap(lambda one_key: jax.random.permutation(one_key, SECTION))(source_keys)[:, :N_CTX]
    phase_perm = phase_perm.reshape(GROUPS, N_CTX, N_CTX)
    coin_flip = jax.random.randint(coin_key, (GROUPS, N_CTX, N_CTX), 0, 2)
    hub_device = jax.random.randint(hub_key, (GROUPS, 1, 1), 0, N_CTX)
    keep_page = (coin_flip == 1) | (jnp.arange(N_CTX)[None, None, :] == hub_device)
    return jnp.where(keep_page, phase_perm, -1).astype(jnp.int32)


def place_ends(values, own_key, smallest, largest):
    longest = values.shape.index(max(values.shape))
    spots = []
    for shift in (0, 1):
        where = [jax.random.randint(jax.random.fold_in(own_key, axis), (), 0, length) for axis, length in enumerate(values.shape)]
        where[longest] = (where[longest] + shift) % values.shape[longest]
        spots.append(tuple(where))
    return values.at[spots[0]].set(smallest).at[spots[1]].set(largest)


def block_scale(key, dims, cuts, smallest, high):
    def one(dim, parts):
        heights = jax.random.uniform(jax.random.fold_in(jax.random.fold_in(key, 6), dim), (parts,), jnp.float32, smallest / len(cuts), high / len(cuts))
        return jnp.repeat(jnp.exp(heights), dims[dim] // parts).reshape((-1,) + (1,) * (len(dims) - dim - 1))

    gain = one(*cuts[0])
    for cut in cuts[1:]:
        gain = gain * one(*cut)
    return gain


def shared_out(own_key, own, number, rows, count, top, reach, lean):
    sequence = jax.random.permutation(own_key, count)
    heavy_load, usual = load_shares(count, rows * top, reach, lean, True), load_shares(count, rows * top, reach, lean, False)
    places = jnp.arange(count)

    def named(lengths, rotation):
        used = int((lengths > 0).sum())
        fixed = max(1, used // 4)
        moved = fixed + (places - fixed + rotation * (used - fixed)) % max(1, count - fixed)
        return jnp.zeros((count,), jnp.int32).at[sequence[jnp.where(places < fixed, places, moved)]].set(jnp.asarray(lengths, jnp.int32))

    lengths = jnp.where(number % 4 == 0, named(heavy_load, number // 4), named(usual, number - number // 4 - 1))
    mixed = jax.random.permutation(jax.random.fold_in(own, 3), count)
    giver, taker = mixed[0:count // 2 * 2:2], mixed[1:count // 2 * 2:2]
    margin = jnp.minimum(lengths[giver] - 1, reach - lengths[taker]) // 2
    margin = jnp.where((giver == sequence[0]) | (taker == sequence[0]) | (lengths[taker] == 0), 0, jnp.maximum(margin, 0))
    moved = jax.random.randint(jax.random.fold_in(own, 4), (count // 2,), 0, 1 << 20) % (margin + 1)
    lengths = lengths.at[giver].add(-moved).at[taker].add(moved)
    members = jnp.searchsorted(jnp.cumsum(lengths), jnp.arange(rows * top), side="right").astype(jnp.int32)
    listing = members.reshape(top, rows).T
    listing = listing[jax.random.permutation(jax.random.fold_in(own, 1), rows)]
    rotation = jax.random.randint(jax.random.fold_in(own, 2), (rows, 1), 0, top)
    return jnp.take_along_axis(listing, (jnp.arange(top)[None, :] + rotation) % top, axis=1)


def load_shares(count, total, bound, skew, full):
    weights = [(1 << 20) // math.isqrt(rank ** skew) + 1 for rank in range(1, count + 1)]
    largest = bound if full else min(bound, max(-(-total // count), total * weights[0] // sum(weights)))
    least = 1 if total - largest >= count - 1 else 0
    counts, spare = [largest] + [least] * (count - 1), total - largest - least * (count - 1)
    while spare > 0:
        movable = [i for i in range(1, count) if counts[i] < largest] or [i for i in range(1, count) if counts[i] < bound]
        whole, budget = sum([weights[i] for i in movable]), spare
        for i in movable:
            more = min(bound - counts[i], max(1, budget * weights[i] // whole), spare)
            counts[i] = counts[i] + more
            spare = spare - more
    return np.array(counts)


def normal_values(own_key, dims, deviation, reach, pieces=(), held_as=jnp.bfloat16):
    values = deviation * jax.random.normal(own_key, dims, jnp.float32)
    if pieces:
        values = values * block_scale(own_key, dims, pieces, -0.22, 0.18)
    return jnp.clip(values, -reach, reach).astype(held_as)


def setup_inputs(seed: int = 0) -> dict:
    splits = jax.random.split(jax.random.key(seed), 18)
    kv_cache = draw_kv_cache(jax.random.fold_in(splits[17], 71), 0)
    slot_owner = draw_slot_owner(jax.random.fold_in(splits[17], 71), 0)
    slot_fill = place_ends(jax.random.randint(splits[2], (GROUPS, CTX_SLOTS), 1, PAGE + 1), jax.random.fold_in(splits[2], 1), 1, PAGE).astype(jnp.int32)
    phased = draw_phased(jax.random.fold_in(splits[17], 71), 0)
    phase_owner = place_ends(jax.random.randint(splits[4], (GROUPS, CTX_SECTION), 0, REQ_DEV), jax.random.fold_in(splits[4], 1), 0, REQ_DEV - 1).astype(jnp.int32)
    phase_fill = place_ends(jax.random.randint(splits[5], (GROUPS, CTX_SECTION), 1, PAGE + 1), jax.random.fold_in(splits[5], 1), 1, PAGE).astype(jnp.int32)
    relay_page = draw_relay_page(jax.random.fold_in(splits[17], 71), 0)
    relay_slot = draw_relay_slot(jax.random.fold_in(splits[17], 71), 0)
    queries = draw_queries(jax.random.fold_in(splits[17], 71), 0)
    new_kv = draw_new_kv(jax.random.fold_in(splits[17], 71), 0)
    hidden_in = draw_hidden_in(jax.random.fold_in(splits[17], 71), 0)
    o_proj = normal_values(splits[11], (QW, D), HEAD ** -0.5, 0.5, ((0, 8), (1, 32)))
    expert_ids_keys = jax.random.split(jax.random.fold_in(splits[12], 1), STEPS * REQS * DRAFT // (REQ_DEV * DRAFT))
    expert_ids_turns = jax.random.permutation(jax.random.fold_in(splits[12], 3), STEPS * REQS * DRAFT // (REQ_DEV * DRAFT))
    expert_ids = jax.vmap(lambda own, number: shared_out(jax.random.fold_in(splits[12], 2), own, number, REQ_DEV * DRAFT, EXPERTS, TOPK, CAP, 1))(expert_ids_keys, expert_ids_turns).reshape((STEPS, REQS, DRAFT, TOPK))
    gate_weights = jnp.clip(0.05 + 0.95 * jax.random.uniform(splits[13], (STEPS, REQS, DRAFT, TOPK), jnp.float32) ** block_scale(splits[13], (STEPS, REQS, DRAFT, TOPK), ((1, 32),), -0.2, 0.2), 0.05, 1.0)
    w_gate = normal_values(splits[14], (EXPERTS, D, FF), D ** -0.5, 0.09375, ((0, 32), (2, 8)))
    w_up = normal_values(splits[15], (EXPERTS, D, FF), D ** -0.5, 0.09375, ((0, 32), (2, 8)))
    w_down = normal_values(splits[16], (EXPERTS, FF, D), FF ** -0.5, 0.15625, ((0, 32), (1, 8)))
    return {"kv_cache": kv_cache, "slot_owner": slot_owner, "slot_fill": slot_fill, "phased": phased, "phase_owner": phase_owner, "phase_fill": phase_fill, "relay_page": relay_page, "relay_slot": relay_slot, "queries": queries, "new_kv": new_kv, "hidden_in": hidden_in, "o_proj": o_proj, "expert_ids": expert_ids, "gate_weights": gate_weights, "w_gate": w_gate, "w_up": w_up, "w_down": w_down}


masked_score = -1e+30
norm_epsilon = 1e-06

def round_trip(values_in):
    return lax.optimization_barrier(values_in.astype(jnp.bfloat16)).astype(jnp.float32)

def relay_group(cache_now, owner_now, fill_now, phase_pages, phase_owner, phase_fill, plan_page, plan_slot):
    source = jnp.arange(N_CTX, dtype=jnp.int32)[:, None]
    destination = jnp.arange(N_CTX, dtype=jnp.int32)[None, :]
    moved = plan_page >= 0
    target = jnp.where(moved, destination * SLOTS + plan_slot, N_CTX * SLOTS).reshape(-1).astype(jnp.int32)
    anchor = (source * SECTION + jnp.maximum(plan_page, 0)).reshape(-1).astype(jnp.int32)
    cache_now = cache_now.at[target].set(phase_pages[anchor], mode='drop')
    owner_now = owner_now.at[target].set(phase_owner[anchor], mode='drop')
    fill_now = fill_now.at[target].set(phase_fill[anchor], mode='drop')
    return (cache_now, owner_now, fill_now)

def attend_group(cache_now, owner_now, fill_now, query_all, fresh_all):
    group_size = HEADS // KV_HEADS
    score_scale = HEAD ** (-0.5)
    page_count = cache_now.shape[0]
    key_heads = cache_now[:, 0].astype(jnp.float32).reshape(page_count, PAGE, KV_HEADS, HEAD)
    value_heads = cache_now[:, 1].astype(jnp.float32).reshape(page_count, PAGE, KV_HEADS, HEAD)
    live_mask = (owner_now >= 0)[:, None] & (jnp.arange(PAGE)[None, :] < fill_now[:, None])
    slot_request = jnp.maximum(owner_now, 0).astype(jnp.int32)
    draft_index = jnp.arange(DRAFT)
    results = []
    for step_index in range(STEPS):
        query_rows = query_all[step_index].astype(jnp.float32).reshape(REQ_DEV, DRAFT, KV_HEADS, group_size, HEAD)
        chosen = query_rows[slot_request]
        scores = jnp.einsum('sqkgd,stkd->sqkgt', chosen, key_heads) * score_scale
        scores = jnp.where(live_mask[:, None, None, None, :], scores, masked_score)
        recent = fresh_all[:step_index + 1].astype(jnp.float32)
        recent_keys = recent[:, :, :, 0].reshape(step_index + 1, REQ_DEV, DRAFT, KV_HEADS, HEAD)
        recent_values = recent[:, :, :, 1].reshape(step_index + 1, REQ_DEV, DRAFT, KV_HEADS, HEAD)
        allowed = (jnp.arange(step_index + 1)[None, :, None] < step_index) | (draft_index[None, None, :] <= draft_index[:, None, None])
        fresh_scores = jnp.einsum('rqkgd,nrjkd->rqkgnj', query_rows, recent_keys) * score_scale
        fresh_scores = jnp.where(allowed[None, :, None, None], fresh_scores, masked_score)
        highest = jax.ops.segment_max(lax.optimization_barrier(jnp.max(scores, axis=-1)), slot_request, num_segments=REQ_DEV)
        highest = jnp.maximum(highest, lax.optimization_barrier(jnp.max(fresh_scores, axis=(-2, -1))))
        probs = jnp.where(live_mask[:, None, None, None, :], jnp.exp(scores - highest[slot_request][..., None]), 0.0)
        fresh_probs = jnp.where(allowed[None, :, None, None], jnp.exp(fresh_scores - highest[..., None, None]), 0.0)
        total_mass = jax.ops.segment_sum(lax.optimization_barrier(jnp.sum(probs, axis=-1)), slot_request, num_segments=REQ_DEV)
        total_mass = total_mass + lax.optimization_barrier(jnp.sum(fresh_probs, axis=(-2, -1)))
        page_sum = jnp.einsum('sqkgt,stkd->sqkgd', round_trip(probs), value_heads)
        accumulated = jax.ops.segment_sum(page_sum, slot_request, num_segments=REQ_DEV)
        accumulated = accumulated + jnp.einsum('rqkgnj,nrjkd->rqkgd', round_trip(fresh_probs), recent_values)
        attended = (accumulated / total_mass[..., None]).reshape(REQ_DEV, DRAFT, HEADS * HEAD)
        results.append(attended.astype(jnp.bfloat16))
    return jnp.stack(results)

def experts_step(normed, expert_row, gate_row, w_gate, w_up, w_down):
    row_count = normed.shape[0]
    flat_ids = expert_row.reshape(-1).astype(jnp.int32)
    hit_table = (flat_ids[:, None] == jnp.arange(EXPERTS, dtype=jnp.int32)[None, :]).astype(jnp.int32)
    blocks = hit_table.reshape(N_EXP, REQ_DEV * DRAFT * TOPK, EXPERTS)
    before = ((jnp.cumsum(blocks, axis=1) - blocks) * blocks).astype(jnp.int32)
    rank_pos = lax.optimization_barrier(jnp.sum(before, axis=-1)).reshape(-1).astype(jnp.int32)
    row_index = (jnp.arange(row_count * TOPK, dtype=jnp.int32) // TOPK).astype(jnp.int32)
    position = (row_index // (REQ_DEV * DRAFT) * CAP + rank_pos).astype(jnp.int32)
    token_index = jnp.zeros((EXPERTS, N_EXP * CAP), jnp.int32).at[flat_ids, position].set(row_index)
    gathered = normed[token_index]

    def run_expert(operands):
        rows_in, gate_w, up_w, down_w = operands
        gate_act = jnp.dot(rows_in, gate_w, preferred_element_type=jnp.float32)
        up_act = jnp.dot(rows_in, up_w, preferred_element_type=jnp.float32)
        hidden_units = (jax.nn.silu(gate_act) * up_act).astype(jnp.bfloat16)
        return jnp.dot(hidden_units, down_w, preferred_element_type=jnp.float32)
    expert_out = lax.map(run_expert, (gathered, w_gate, w_up, w_down))
    picked = expert_out[flat_ids, position].astype(jnp.float32).reshape(row_count, TOPK, -1)
    mixing = gate_row / lax.optimization_barrier(jnp.sum(gate_row, axis=-1, keepdims=True))
    return lax.optimization_barrier(jnp.sum(mixing[..., None] * picked, axis=1))

def reference(kv_cache, slot_owner, slot_fill, phased, phase_owner, phase_fill, relay_page, relay_slot, queries, new_kv, hidden_in, o_proj, expert_ids, gate_weights, w_gate, w_up, w_down):
    query_groups = queries.reshape(STEPS, N_EXP, REQ_DEV, DRAFT, HEADS * HEAD).transpose(1, 0, 2, 3, 4)
    fresh_groups = new_kv.reshape(STEPS, N_EXP, REQ_DEV, DRAFT, 2, KV_HEADS * HEAD).transpose(1, 0, 2, 3, 4, 5)

    def per_group(operands):
        cache_now, owner_now, fill_now, phase_pages, owner_phase, fill_phase, plan_page, plan_slot, query_all, fresh_all = operands
        cache_now, owner_now, fill_now = relay_group(cache_now, owner_now, fill_now, phase_pages, owner_phase, fill_phase, plan_page, plan_slot)
        return attend_group(cache_now, owner_now, fill_now, query_all, fresh_all)
    attended = lax.map(per_group, (kv_cache, slot_owner, slot_fill, phased, phase_owner, phase_fill, relay_page, relay_slot, query_groups, fresh_groups))
    attended = attended.transpose(1, 0, 2, 3, 4).reshape(STEPS, N_EXP * REQ_DEV * DRAFT, HEADS * HEAD)
    results = []
    for step_index in range(STEPS):
        projected = jnp.dot(attended[step_index], o_proj, preferred_element_type=jnp.float32)
        residual = hidden_in[step_index].reshape(-1, D).astype(jnp.float32) + projected
        normed = (residual * lax.rsqrt(lax.optimization_barrier(jnp.mean(residual * residual, axis=-1, keepdims=True)) + norm_epsilon)).astype(jnp.bfloat16)
        mixed_part = experts_step(normed, expert_ids[step_index].reshape(-1, TOPK), gate_weights[step_index].reshape(-1, TOPK), w_gate, w_up, w_down)
        results.append((residual + mixed_part).astype(jnp.bfloat16).reshape(N_EXP * REQ_DEV, DRAFT, D))
    return jnp.stack(results)
```

```python
import functools

import jax
import jax.numpy as jnp
from jax import lax
from jax.experimental import pallas as pl
from jax.experimental.pallas import tpu as pltpu
from jax.sharding import Mesh, PartitionSpec as P

HEADS = 64
KV_HEADS = 4
HEAD = 128
TOPK = 8
NY, NCORE, NZ, NX = 4, 2, 8, 4
NC = NY * NCORE
ROWS = 48
ALL = NX * ROWS
KEYS = 1152
CAP = 6
SLOTS = NZ * 2 * NX * 2 * CAP
WIDTH = 4096
COLS = WIDTH // NC
FFS = 192
SCALE = HEAD ** (-0.5)
EPS = 1e-06
MASKED = -1e30
CTX = ("y", "core")
BF = jnp.bfloat16
F32 = jnp.float32


def params(mb=40):
    return pltpu.CompilerParams(vmem_limit_bytes=mb * 1024 * 1024)


def dot(a, b, dims=((1,), (0,))):
    return lax.dot_general(a, b, (dims, ((), ())), preferred_element_type=F32)


def thresholds(value, step, count):
    total = jnp.zeros_like(value)
    for n in range(1, count):
        total = total + (value >= n * step).astype(value.dtype)
    return total


def attention_kernel(
    place, owner, fill, phase_owner, phase_fill, relay, q, kv, ph, fk, fv, out, bias, keys, vals
):
    @pl.when(pl.program_id(0) == 0)
    def _():
        me = place[0]
        key = lax.broadcasted_iota(jnp.int32, (8, KEYS), 1)
        page = lax.shift_right_logical(key, 5)
        own = jnp.full((8, KEYS), -1, jnp.int32)
        cap = jnp.zeros((8, KEYS), jnp.int32)
        for p in range(24):
            own = jnp.where(page == p, owner[0, p], own)
            cap = jnp.where(page == p, fill[0, p], cap)
        for p in range(8):
            sent = relay[me, 0] == p
            for d in range(1, NC):
                sent = sent | (relay[me, d] == p)
            at = me * 8 + p
            own = jnp.where(page == 24 + p, jnp.where(sent, phase_owner[0, at], -1), own)
            cap = jnp.where(page == 24 + p, phase_fill[0, at], cap)
        own = jnp.where((key & 31) < cap, own, -1)[0:1]
        row = lax.broadcasted_iota(jnp.int32, (ROWS, KEYS), 0)
        step = thresholds(row, 24, 2)
        rest = row - 24 * step
        req = thresholds(rest, 6, 4)
        draft = rest - 6 * req
        fresh = lax.broadcasted_iota(jnp.int32, (ROWS, KEYS), 1) - 1024
        f_step = thresholds(fresh, 24, 2)
        f_rest = fresh - 24 * f_step
        f_req = thresholds(f_rest, 6, 4)
        f_draft = f_rest - 6 * f_req
        earlier = (f_step < step) | ((f_step == step) & (f_draft <= draft))
        is_fresh = (fresh >= 0) & (fresh < ROWS) & (f_req == req) & earlier
        is_fresh = is_fresh & (jnp.full((ROWS, KEYS), me, jnp.int32) == 0)
        seen = (jnp.broadcast_to(own, (ROWS, KEYS)) == req) | is_fresh
        bias[...] = jnp.where(seen, 0.0, MASKED)
        keys[1024 + ROWS :, :] = jnp.zeros((KEYS - 1024 - ROWS, HEAD), BF)
        vals[1024 + ROWS :, :] = jnp.zeros((KEYS - 1024 - ROWS, HEAD), BF)

    keys[0:768, :] = kv[:, 0].reshape(768, HEAD)
    keys[768:1024, :] = ph[:, 0].reshape(256, HEAD)
    keys[1024 : 1024 + ROWS, :] = fk[...]
    vals[0:768, :] = kv[:, 1].reshape(768, HEAD)
    vals[768:1024, :] = ph[:, 1].reshape(256, HEAD)
    vals[1024 : 1024 + ROWS, :] = fv[...]
    lane = lax.broadcasted_iota(jnp.int32, (ROWS, HEAD), 1)
    for half in range(2):
        ext = jnp.zeros((ROWS, HEAD), F32)
        for h0 in range(0, 8, 4):
            parts = []
            for h in range(h0, h0 + 4):
                g = half * 8 + h
                parts.append(q[:, g * HEAD : (g + 1) * HEAD])
            qs = jnp.concatenate(parts, axis=0)
            s = dot(qs, keys[...], ((1,), (1,)))
            s = (s.reshape(4, ROWS, KEYS) + bias[...][None]).reshape(4 * ROWS, KEYS)
            top = jnp.max(s, axis=-1, keepdims=True)
            p = jnp.exp((s - top) * SCALE)
            mass = jnp.sum(p, axis=-1, keepdims=True)
            o = dot(p.astype(BF), vals[...]) / mass
            for n in range(4):
                h = h0 + n
                rows = slice(n * ROWS, (n + 1) * ROWS)
                out[half, :, h * HEAD : (h + 1) * HEAD] = o[rows].astype(BF)
                ext = jnp.where(lane == h, top[rows], ext)
                ext = jnp.where(lane == 64 + h, mass[rows], ext)
        high = ext.astype(BF).astype(F32)
        rest = ext - high
        mid = rest.astype(BF).astype(F32)
        low = rest - mid
        packed = high + pltpu.roll(mid, 8, 1) + pltpu.roll(low, 16, 1)
        out[half, :, 8 * HEAD : 9 * HEAD] = packed.astype(BF)


def attention(place, owner, fill, phase_owner, phase_fill, relay, q, kv, ph, fresh):
    smem = pl.BlockSpec(memory_space=pltpu.SMEM)
    return pl.pallas_call(
        attention_kernel,
        grid=(KV_HEADS,),
        in_specs=[smem] * 6
        + [
            pl.BlockSpec((ROWS, 16 * HEAD), lambda k: (0, k)),
            pl.BlockSpec((24, 2, 32, HEAD), lambda k: (0, 0, 0, k)),
            pl.BlockSpec((8, 2, 32, HEAD), lambda k: (0, 0, 0, k)),
            pl.BlockSpec((ROWS, HEAD), lambda k: (0, k)),
            pl.BlockSpec((ROWS, HEAD), lambda k: (0, KV_HEADS + k)),
        ],
        out_specs=pl.BlockSpec((2, ROWS, 9 * HEAD), lambda k: (k, 0, 0)),
        out_shape=jax.ShapeDtypeStruct((NC, ROWS, 9 * HEAD), BF),
        scratch_shapes=[
            pltpu.VMEM((ROWS, KEYS), F32),
            pltpu.VMEM((KEYS, HEAD), BF),
            pltpu.VMEM((KEYS, HEAD), BF),
        ],
        compiler_params=params(),
        name="attention",
    )(place, owner, fill, phase_owner, phase_fill, relay, q, kv, ph, fresh, fresh)


def join_kernel(parts, out):
    tops, masses = [], []
    for c in range(NC):
        ext = parts[c, :, 8 * HEAD :].astype(F32)
        ext = ext + pltpu.roll(ext, HEAD - 8, 1) + pltpu.roll(ext, HEAD - 16, 1)
        tops.append(ext)
        masses.append(pltpu.roll(ext, 64, 1))
    best = functools.reduce(jnp.maximum, tops)
    weights = [m * jnp.exp((t - best) * SCALE) for t, m in zip(tops, masses)]
    total = functools.reduce(jnp.add, weights)
    shares = [w / total for w in weights]
    for h in range(8):
        cols = slice(h * HEAD, (h + 1) * HEAD)
        acc = shares[0][:, h : h + 1] * parts[0, :, cols].astype(F32)
        for c in range(1, NC):
            acc = acc + shares[c][:, h : h + 1] * parts[c, :, cols].astype(F32)
        out[:, cols] = acc.astype(BF)


def join(parts):
    return pl.pallas_call(
        join_kernel,
        out_shape=jax.ShapeDtypeStruct((ROWS, 8 * HEAD), BF),
        compiler_params=params(),
        name="join",
    )(parts)


def project_kernel(place, a0, a1, a2, a3, w, out, rows):
    @pl.when(pl.program_id(0) == 0)
    def _():
        for d, a in enumerate((a0, a1, a2, a3)):
            at = pl.multiple_of(lax.rem(place[1] + d, NX) * ROWS, 16)
            rows[pl.ds(at, ROWS), :] = a[...]

    for n in range(2):
        out[n] = dot(rows[...], w[n]).astype(BF)


def project(place, pieces, w):
    whole = pl.BlockSpec((ROWS, 8 * HEAD), lambda k: (0, 0))
    return pl.pallas_call(
        project_kernel,
        grid=(NZ // 2,),
        in_specs=[pl.BlockSpec(memory_space=pltpu.SMEM)]
        + [whole] * 4
        + [pl.BlockSpec((2, 8 * HEAD, HEAD), lambda k: (k, 0, 0))],
        out_specs=pl.BlockSpec((2, ALL, HEAD), lambda k: (k, 0, 0)),
        out_shape=jax.ShapeDtypeStruct((NZ, ALL, HEAD), BF),
        scratch_shapes=[pltpu.VMEM((ALL, 8 * HEAD), BF)],
        compiler_params=params(),
        name="project",
    )(place, *pieces, w)


def add_kernel(parts, out):
    acc = parts[0].astype(F32)
    for c in range(1, NC):
        acc = acc + parts[c].astype(F32)
    out[...] = acc.astype(BF)


def add_up(parts):
    return pl.pallas_call(
        add_kernel,
        out_shape=jax.ShapeDtypeStruct((ALL, HEAD), BF),
        compiler_params=params(),
        name="add_up",
    )(parts)


def floor_div(value, by):
    return jnp.floor((value + 0.5) * (1.0 / by))


def slot_fields(value):
    z = floor_div(value, 96)
    rest = value - 96 * z
    ex = floor_div(rest, 48)
    rest = rest - 48 * ex
    block = floor_div(rest, CAP)
    spot = rest - CAP * block
    return z, ex, block, spot


def routes_kernel(place, t0, t1, t2, t3, send, mix_high, mix_low, ids, gates):
    for d, t in enumerate((t0, t1, t2, t3)):
        at = pl.multiple_of(lax.rem(place[1] + d, NX) * ROWS, 16)
        ids[pl.ds(at, ROWS), :] = t[0]
        gates[pl.ds(at, ROWS), :] = t[1]
    x_here = place[1].astype(F32)
    expert = lax.broadcasted_iota(jnp.int32, (ALL, 64), 1).astype(F32)
    gate_rows = gates[...]
    share = gate_rows / jnp.sum(gate_rows, axis=-1, keepdims=True)
    id_rows = ids[...]
    hit = jnp.zeros((ALL, 64), F32)
    mix = jnp.zeros((ALL, 64), F32)
    for k in range(TOPK):
        same = id_rows[:, k : k + 1] == expert
        hit = jnp.where(same, 1.0, hit)
        mix = jnp.where(same, share[:, k : k + 1], mix)
    row_a = lax.broadcasted_iota(jnp.int32, (ALL, ALL), 0).astype(F32)
    row_b = lax.broadcasted_iota(jnp.int32, (ALL, ALL), 1).astype(F32)
    earlier = (row_b < row_a) & (floor_div(row_a, 24) == floor_div(row_b, 24))
    before = dot(jnp.where(earlier, 1.0, 0.0).astype(BF), hit.astype(BF))
    mark = jnp.where(hit > 0, before + 1.0, 0.0).astype(BF)
    mix_a = mix.astype(BF)
    mix_b = (mix - mix_a.astype(F32)).astype(BF)

    slot = lax.broadcasted_iota(jnp.int32, (SLOTS, 64), 0).astype(F32)
    z, ex, _, _ = slot_fields(slot)
    e_here = lax.broadcasted_iota(jnp.int32, (SLOTS, 64), 1).astype(F32)
    pick = jnp.where(e_here == 8 * z + 2 * x_here + ex, 1.0, 0.0).astype(BF)
    marked = dot(pick, mark, ((1,), (1,)))
    slot = lax.broadcasted_iota(jnp.int32, (SLOTS, ALL), 0).astype(F32)
    _, _, block, spot = slot_fields(slot)
    row = lax.broadcasted_iota(jnp.int32, (SLOTS, ALL), 1).astype(F32)
    chosen = (marked == spot + 1.0) & (floor_div(row, 24) == block)
    send[...] = jnp.where(chosen, 1.0, 0.0).astype(BF)

    slot = lax.broadcasted_iota(jnp.int32, (64, SLOTS), 1).astype(F32)
    z, ex, _, _ = slot_fields(slot)
    e_here = lax.broadcasted_iota(jnp.int32, (64, SLOTS), 0).astype(F32)
    pick = jnp.where(e_here == 8 * z + 2 * x_here + ex, 1.0, 0.0).astype(BF)
    marked = dot(mark, pick)
    slot = lax.broadcasted_iota(jnp.int32, (ALL, SLOTS), 1).astype(F32)
    _, _, block, spot = slot_fields(slot)
    row = lax.broadcasted_iota(jnp.int32, (ALL, SLOTS), 0).astype(F32)
    chosen = (marked == spot + 1.0) & (floor_div(row, 24) == block)
    mix_high[...] = jnp.where(chosen, dot(mix_a, pick), 0.0).astype(BF)
    mix_low[...] = jnp.where(chosen, dot(mix_b, pick), 0.0).astype(BF)


def routes(place, tables):
    vm = pl.BlockSpec(memory_space=pltpu.VMEM)
    return pl.pallas_call(
        routes_kernel,
        in_specs=[pl.BlockSpec(memory_space=pltpu.SMEM)] + [vm] * 4,
        out_specs=[vm] * 3,
        out_shape=[
            jax.ShapeDtypeStruct((SLOTS, ALL), BF),
            jax.ShapeDtypeStruct((ALL, SLOTS), BF),
            jax.ShapeDtypeStruct((ALL, SLOTS), BF),
        ],
        scratch_shapes=[pltpu.VMEM((ALL, TOPK), F32), pltpu.VMEM((ALL, TOPK), F32)],
        compiler_params=params(),
        name="routes",
    )(place, *tables)


def dispatch_kernel(place, h0, h1, h2, h3, p0, p1, p2, p3, send, packed, mine, rows):
    for d, (h, p) in enumerate(zip((h0, h1, h2, h3), (p0, p1, p2, p3))):
        there = lax.rem(place[1] + d, NX)
        at = pl.multiple_of(there * ROWS, 16)
        rows[pl.ds(at, ROWS), :] = h[...].astype(F32)
    for d, p in enumerate((p0, p1, p2, p3)):
        at = pl.multiple_of(lax.rem(place[1] + d, NX) * HEAD, HEAD)
        rows[:, pl.ds(at, HEAD)] = rows[:, pl.ds(at, HEAD)] + p[...].astype(F32)
    mine[...] = rows[pl.ds(pl.multiple_of(place[1] * ROWS, 16), ROWS), :]
    packed[...] = dot(send[...], rows[...].astype(BF)).astype(BF)


def dispatch(place, hidden, projected, send):
    vm = pl.BlockSpec(memory_space=pltpu.VMEM)
    return pl.pallas_call(
        dispatch_kernel,
        in_specs=[pl.BlockSpec(memory_space=pltpu.SMEM)] + [vm] * 9,
        out_specs=[vm] * 2,
        out_shape=[
            jax.ShapeDtypeStruct((SLOTS, COLS), BF),
            jax.ShapeDtypeStruct((ROWS, COLS), F32),
        ],
        scratch_shapes=[pltpu.VMEM((ALL, COLS), F32)],
        compiler_params=params(),
        name="dispatch",
    )(place, *hidden, *projected, send)


def up_kernel(x, wg, wu, out, gate, up, square):
    c = pl.program_id(1)
    rows = x[...].reshape(NZ * ROWS, COLS)
    part_gate = dot(rows, wg[0])
    part_up = dot(rows, wu[0])
    wide = rows.astype(F32)
    part_square = jnp.sum(wide * wide, axis=-1, keepdims=True)

    @pl.when(c == 0)
    def _():
        gate[...] = part_gate
        up[...] = part_up
        square[...] = part_square

    @pl.when(c > 0)
    def _():
        gate[...] += part_gate
        up[...] += part_up
        square[...] += part_square

    @pl.when(c == NC - 1)
    def _():
        scale = lax.rsqrt(square[...] * (1.0 / WIDTH) + EPS)
        v = gate[...] * scale
        out[0] = (v / (1.0 + jnp.exp(-v)) * (up[...] * scale)).astype(BF)


def expert_up(x, wg, wu):
    n = NZ * ROWS
    return pl.pallas_call(
        up_kernel,
        grid=(2, NC),
        in_specs=[
            pl.BlockSpec((1, NZ, 1, ROWS, COLS), lambda e, c: (c, 0, e, 0, 0)),
            pl.BlockSpec((1, COLS, FFS), lambda e, c: (e, c, 0)),
            pl.BlockSpec((1, COLS, FFS), lambda e, c: (e, c, 0)),
        ],
        out_specs=pl.BlockSpec((1, n, FFS), lambda e, c: (e, 0, 0)),
        out_shape=jax.ShapeDtypeStruct((2, n, FFS), BF),
        scratch_shapes=[pltpu.VMEM((n, FFS), F32), pltpu.VMEM((n, FFS), F32), pltpu.VMEM((n, 1), F32)],
        compiler_params=params(),
        name="expert_up",
    )(x, wg, wu)


def down_kernel(h, w, out):
    acc = dot(h[0, 0], w[0, 0])
    for c in range(1, NC):
        acc = acc + dot(h[c, 0], w[c, 0])
    out[...] = acc.astype(BF).reshape(NZ, 1, ROWS, COLS)


def expert_down(h, w):
    n = NZ * ROWS
    return pl.pallas_call(
        down_kernel,
        grid=(2,),
        in_specs=[
            pl.BlockSpec((NC, 1, n, FFS), lambda e: (0, e, 0, 0)),
            pl.BlockSpec((NC, 1, FFS, COLS), lambda e: (0, e, 0, 0)),
        ],
        out_specs=pl.BlockSpec((NZ, 1, ROWS, COLS), lambda e: (0, e, 0, 0)),
        out_shape=jax.ShapeDtypeStruct((NZ, 2, ROWS, COLS), BF),
        compiler_params=params(),
        name="expert_down",
    )(h, w)


def mix_kernel(place, back, mix_high, mix_low, o0, o1, o2, o3, rows):
    rows[...] = dot(mix_high[...], back[...]) + dot(mix_low[...], back[...])
    for d, o in enumerate((o0, o1, o2, o3)):
        at = pl.multiple_of(lax.rem(place[1] + d, NX) * ROWS, 16)
        o[...] = rows[pl.ds(at, ROWS), :].astype(o.dtype)


def mix_back(place, back, mix_high, mix_low):
    vm = pl.BlockSpec(memory_space=pltpu.VMEM)
    return pl.pallas_call(
        mix_kernel,
        in_specs=[pl.BlockSpec(memory_space=pltpu.SMEM)] + [vm] * 3,
        out_specs=[vm] * 4,
        out_shape=[jax.ShapeDtypeStruct((ROWS, COLS), F32)]
        + [jax.ShapeDtypeStruct((ROWS, COLS), BF)] * 3,
        scratch_shapes=[pltpu.VMEM((ALL, COLS), F32)],
        compiler_params=params(),
        name="mix_back",
    )(place, back, mix_high, mix_low)


def from_x(value, d):
    return lax.ppermute(value, "x", [((i + d) % NX, i) for i in range(NX)])


def along_x(value):
    return [value] + [from_x(value, d) for d in range(1, NX)]


def body(
    kv_cache,
    slot_owner,
    slot_fill,
    phased,
    phase_owner,
    phase_fill,
    relay_page,
    relay_slot,
    queries,
    new_kv,
    hidden_in,
    o_proj,
    expert_ids,
    gate_weights,
    w_gate,
    w_up,
    w_down,
):
    del relay_slot
    ctx = lax.axis_index(CTX)
    place = jnp.stack([ctx, lax.axis_index("x")]).astype(jnp.int32)

    with jax.named_scope("gather_projection"):
        o_cols = lax.all_gather(o_proj, "z")
    with jax.named_scope("gather_tables"):
        table = jnp.stack(
            [expert_ids.reshape(ROWS, TOPK).astype(F32), gate_weights.reshape(ROWS, TOPK)]
        )
        tables = along_x(table)
    with jax.named_scope("gather_hidden"):
        hidden_cols = lax.dynamic_slice_in_dim(hidden_in, ctx * COLS, COLS, 3).reshape(ROWS, COLS)
        hidden = along_x(hidden_cols)
    with jax.named_scope("turn_down"):
        down_cols = lax.all_to_all(
            w_down.reshape(2, FFS, NC, COLS).transpose(2, 0, 1, 3), CTX, 0, 0, tiled=True
        )

    with jax.named_scope("attend"):
        parts = attention(
            place,
            slot_owner,
            slot_fill,
            phase_owner,
            phase_fill,
            relay_page[0],
            queries.reshape(ROWS, HEADS * HEAD),
            kv_cache[0],
            phased[0],
            new_kv.reshape(ROWS, 2 * KV_HEADS * HEAD),
        )
    with jax.named_scope("join_parts"):
        parts = lax.all_to_all(parts, CTX, 0, 0, tiled=True)
        attended = join(parts)
    with jax.named_scope("project_rows"):
        partial = project(place, along_x(attended), o_cols)
    with jax.named_scope("sum_projection"):
        columns = add_up(lax.all_to_all(partial, CTX, 0, 0, tiled=True))
        projected = along_x(columns)
    with jax.named_scope("find_routes"):
        send, mix_high, mix_low = routes(place, tables)
    with jax.named_scope("dispatch_rows"):
        packed, mine = dispatch(place, hidden, projected, send)
        arrived = lax.all_to_all(packed.reshape(NZ, 96, COLS), "z", 0, 0, tiled=True)
    with jax.named_scope("gather_rows"):
        rows = lax.all_gather(arrived, CTX).reshape(NC, NZ, 2, ROWS, COLS)
    with jax.named_scope("up"):
        units = expert_up(rows, w_gate, w_up)
    with jax.named_scope("gather_units"):
        units = lax.all_gather(units, CTX)
    with jax.named_scope("down"):
        outcome = expert_down(units, down_cols)
    with jax.named_scope("return_rows"):
        back = lax.all_to_all(outcome.reshape(NZ, 96, COLS), "z", 0, 0, tiled=True)
    with jax.named_scope("mix"):
        mixed = mix_back(place, back.reshape(SLOTS, COLS), mix_high, mix_low)
        total = mine + mixed[0]
        for d in range(1, NX):
            total = total + from_x(mixed[d], NX - d).astype(F32)
    return total.astype(BF).reshape(2, 4, 6, COLS)


def solution(mesh):
    inner = Mesh(mesh.devices.reshape(NY, NCORE, NZ, NX), ("y", "core", "z", "x"))
    exp = ("z", "x")
    in_specs = (
        P(exp, CTX, None, None, None),
        P(exp, CTX),
        P(exp, CTX),
        P(exp, CTX, None, None, None),
        P(exp, None),
        P(exp, None),
        P(exp, None, None),
        P(exp, None, None),
        P(None, exp, None, None),
        P(None, exp, None, None, None),
        P(None, exp, None, None),
        P(CTX, exp),
        P(None, exp, None, None),
        P(None, exp, None, None),
        P(exp, None, CTX),
        P(exp, None, CTX),
        P(exp, CTX, None),
    )
    out_specs = P(None, exp, None, CTX)
    return jax.shard_map(body, mesh=inner, in_specs=in_specs, out_specs=out_specs, check_vma=False)
```

```python
import functools

import jax
import jax.numpy as jnp
from jax import lax
from jax.experimental import pallas as pl
from jax.experimental.pallas import tpu as pltpu
from jax.sharding import Mesh, PartitionSpec as P

HEADS = 64
KV_HEADS = 4
HEAD = 128
TOPK = 8
NY, NCORE, NZ, NX = 4, 2, 8, 4
NC = NY * NCORE
ROWS = 48
ALL = NX * ROWS
KEYS = 1152
CAP = 6
EXPERT_ROWS = 384
SLOTS = NZ * 2 * NX * 2 * CAP
WIDTH = 4096
COLS = WIDTH // NC
FFS = 192
SCALE = HEAD ** (-0.5)
EPS = 1e-06
MASKED = -1e30
CTX = ("y", "core")
BF = jnp.bfloat16
F32 = jnp.float32


def params(mb=40):
    return pltpu.CompilerParams(vmem_limit_bytes=mb * 1024 * 1024)


def dot(a, b, dims=((1,), (0,))):
    return lax.dot_general(a, b, (dims, ((), ())), preferred_element_type=F32)


def thresholds(value, step, count):
    total = jnp.zeros_like(value)
    for n in range(1, count):
        total = total + (value >= n * step).astype(value.dtype)
    return total


def attention_kernel(
    place, owner, fill, phase_owner, phase_fill, relay, q, kv, ph, fk, fv, out, bias, keys, vals, qf
):
    @pl.when(pl.program_id(0) == 0)
    def _():
        me = place[0]
        key = lax.broadcasted_iota(jnp.int32, (8, KEYS), 1)
        page = lax.shift_right_logical(key, 5)
        own = jnp.full((8, KEYS), -1, jnp.int32)
        cap = jnp.zeros((8, KEYS), jnp.int32)
        for p in range(24):
            own = jnp.where(page == p, owner[0, p], own)
            cap = jnp.where(page == p, fill[0, p], cap)
        for p in range(8):
            sent = relay[me, 0] == p
            for d in range(1, NC):
                sent = sent | (relay[me, d] == p)
            at = me * 8 + p
            own = jnp.where(page == 24 + p, jnp.where(sent, phase_owner[0, at], -1), own)
            cap = jnp.where(page == 24 + p, phase_fill[0, at], cap)
        own = jnp.where((key & 31) < cap, own, -1)[0:1]
        row = lax.broadcasted_iota(jnp.int32, (ROWS, KEYS), 0)
        step = thresholds(row, 24, 2)
        rest = row - 24 * step
        draft = lax.shift_right_logical(rest, 2)
        req = rest & 3
        fresh = lax.broadcasted_iota(jnp.int32, (ROWS, KEYS), 1) - 1024
        f_step = thresholds(fresh, 24, 2)
        f_rest = fresh - 24 * f_step
        f_req = thresholds(f_rest, 6, 4)
        f_draft = f_rest - 6 * f_req
        earlier = (f_step < step) | ((f_step == step) & (f_draft <= draft))
        is_fresh = (fresh >= 0) & (fresh < ROWS) & (f_req == req) & earlier
        is_fresh = is_fresh & (jnp.full((ROWS, KEYS), me, jnp.int32) == 0)
        seen = (jnp.broadcast_to(own, (ROWS, KEYS)) == req) | is_fresh
        bias[...] = jnp.where(seen, 0.0, MASKED)
        keys[1024 + ROWS :, :] = jnp.zeros((KEYS - 1024 - ROWS, HEAD), BF)
        vals[1024 + ROWS :, :] = jnp.zeros((KEYS - 1024 - ROWS, HEAD), BF)

    keys[0:768, :] = kv[:, 0].reshape(768, HEAD)
    keys[768:1024, :] = ph[:, 0].reshape(256, HEAD)
    keys[1024 : 1024 + ROWS, :] = fk[...]
    vals[0:768, :] = kv[:, 1].reshape(768, HEAD)
    vals[768:1024, :] = ph[:, 1].reshape(256, HEAD)
    vals[1024 : 1024 + ROWS, :] = fv[...]
    for n in range(12):
        qf[n * 4 : n * 4 + 4, :] = q[n // 6, n % 6].astype(F32)
    lane = lax.broadcasted_iota(jnp.int32, (ROWS, HEAD), 1)
    for half in range(2):
        ext = jnp.zeros((ROWS, HEAD), F32)
        for h0 in range(0, 8, 4):
            parts = []
            for h in range(h0, h0 + 4):
                g = half * 8 + h
                parts.append(qf[:, g * HEAD : (g + 1) * HEAD].astype(BF))
            qs = jnp.concatenate(parts, axis=0)
            s = dot(qs, keys[...], ((1,), (1,)))
            s = (s.reshape(4, ROWS, KEYS) + bias[...][None]).reshape(4 * ROWS, KEYS)
            top = jnp.max(s, axis=-1, keepdims=True)
            p = jnp.exp((s - top) * SCALE)
            mass = jnp.sum(p, axis=-1, keepdims=True)
            o = dot(p.astype(BF), vals[...]) / mass
            for n in range(4):
                h = h0 + n
                rows = slice(n * ROWS, (n + 1) * ROWS)
                out[half, :, h * HEAD : (h + 1) * HEAD] = o[rows].astype(BF)
                ext = jnp.where(lane == h, top[rows], ext)
                ext = jnp.where(lane == 64 + h, mass[rows], ext)
        high = ext.astype(BF).astype(F32)
        rest = ext - high
        mid = rest.astype(BF).astype(F32)
        low = rest - mid
        packed = high + pltpu.roll(mid, 8, 1) + pltpu.roll(low, 16, 1)
        out[half, :, 8 * HEAD : 9 * HEAD] = packed.astype(BF)


def attention(place, owner, fill, phase_owner, phase_fill, relay, q, kv, ph, fresh):
    smem = pl.BlockSpec(memory_space=pltpu.SMEM)
    return pl.pallas_call(
        attention_kernel,
        grid=(KV_HEADS,),
        in_specs=[smem] * 6
        + [
            pl.BlockSpec((2, 6, 4, 16 * HEAD), lambda k: (0, 0, 0, k)),
            pl.BlockSpec((24, 2, 32, HEAD), lambda k: (0, 0, 0, k)),
            pl.BlockSpec((8, 2, 32, HEAD), lambda k: (0, 0, 0, k)),
            pl.BlockSpec((ROWS, HEAD), lambda k: (0, k)),
            pl.BlockSpec((ROWS, HEAD), lambda k: (0, KV_HEADS + k)),
        ],
        out_specs=pl.BlockSpec((2, ROWS, 9 * HEAD), lambda k: (k, 0, 0)),
        out_shape=jax.ShapeDtypeStruct((NC, ROWS, 9 * HEAD), BF),
        scratch_shapes=[
            pltpu.VMEM((ROWS, KEYS), F32),
            pltpu.VMEM((KEYS, HEAD), BF),
            pltpu.VMEM((KEYS, HEAD), BF),
            pltpu.VMEM((ROWS, 16 * HEAD), F32),
        ],
        compiler_params=params(62),
        name="attention",
    )(place, owner, fill, phase_owner, phase_fill, relay, q, kv, ph, fresh, fresh)


def join_kernel(parts, out):
    tops, masses = [], []
    for c in range(NC):
        ext = parts[c, :, 8 * HEAD :].astype(F32)
        ext = ext + pltpu.roll(ext, HEAD - 8, 1) + pltpu.roll(ext, HEAD - 16, 1)
        tops.append(ext)
        masses.append(pltpu.roll(ext, 64, 1))
    best = functools.reduce(jnp.maximum, tops)
    weights = [m * jnp.exp((t - best) * SCALE) for t, m in zip(tops, masses)]
    total = functools.reduce(jnp.add, weights)
    shares = [w / total for w in weights]
    for h in range(8):
        cols = slice(h * HEAD, (h + 1) * HEAD)
        acc = shares[0][:, h : h + 1] * parts[0, :, cols].astype(F32)
        for c in range(1, NC):
            acc = acc + shares[c][:, h : h + 1] * parts[c, :, cols].astype(F32)
        out[:, cols] = acc.astype(BF)


def join(parts):
    return pl.pallas_call(
        join_kernel,
        out_shape=jax.ShapeDtypeStruct((ROWS, 8 * HEAD), BF),
        compiler_params=params(),
        name="join",
    )(parts)


def project_kernel(place, a0, a1, a2, a3, w, out, rows):
    @pl.when(pl.program_id(0) == 0)
    def _():
        for d, a in enumerate((a0, a1, a2, a3)):
            at = pl.multiple_of(lax.rem(place[1] + d, NX) * ROWS, 16)
            rows[pl.ds(at, ROWS), :] = a[...]

    for n in range(0, NZ // 2, 2):
        both = dot(rows[...], jnp.concatenate([w[n], w[n + 1]], axis=1)).astype(BF)
        out[n], out[n + 1] = both[:, 0:HEAD], both[:, HEAD:]


def project(place, pieces, w):
    whole = pl.BlockSpec((ROWS, 8 * HEAD), lambda k: (0, 0))
    return pl.pallas_call(
        project_kernel,
        grid=(2,),
        in_specs=[pl.BlockSpec(memory_space=pltpu.SMEM)]
        + [whole] * 4
        + [pl.BlockSpec((NZ // 2, 8 * HEAD, HEAD), lambda k: (k, 0, 0))],
        out_specs=pl.BlockSpec((NZ // 2, ALL, HEAD), lambda k: (k, 0, 0)),
        out_shape=jax.ShapeDtypeStruct((NZ, ALL, HEAD), BF),
        scratch_shapes=[pltpu.VMEM((ALL, 8 * HEAD), BF)],
        compiler_params=params(62),
        name="project",
    )(place, *pieces, w)


def add_kernel(parts, out):
    acc = parts[0].astype(F32)
    for c in range(1, NC):
        acc = acc + parts[c].astype(F32)
    out[...] = acc.astype(BF)


def add_up(parts):
    return pl.pallas_call(
        add_kernel,
        out_shape=jax.ShapeDtypeStruct((ALL, HEAD), BF),
        compiler_params=params(),
        name="add_up",
    )(parts)


def floor_div(value, by):
    return jnp.floor((value + 0.5) * (1.0 / by))


def slot_fields(value):
    z = floor_div(value, 96)
    rest = value - 96 * z
    ex = floor_div(rest, 48)
    rest = rest - 48 * ex
    block = floor_div(rest, CAP)
    spot = rest - CAP * block
    return z, ex, block, spot


def routes_kernel(place, t0, t1, t2, t3, send, mix_high, mix_low, ids, gates):
    for d, t in enumerate((t0, t1, t2, t3)):
        at = pl.multiple_of(lax.rem(place[1] + d, NX) * ROWS, 16)
        ids[pl.ds(at, ROWS), :] = t[0]
        gates[pl.ds(at, ROWS), :] = t[1]
    x_here = place[1].astype(F32)
    expert = lax.broadcasted_iota(jnp.int32, (ALL, 64), 1).astype(F32)
    gate_rows = gates[...]
    share = gate_rows / jnp.sum(gate_rows, axis=-1, keepdims=True)
    id_rows = ids[...]
    hit = jnp.zeros((ALL, 64), F32)
    mix = jnp.zeros((ALL, 64), F32)
    for k in range(TOPK):
        same = id_rows[:, k : k + 1] == expert
        hit = jnp.where(same, 1.0, hit)
        mix = jnp.where(same, share[:, k : k + 1], mix)
    row_a = lax.broadcasted_iota(jnp.int32, (ALL, ALL), 0).astype(F32)
    row_b = lax.broadcasted_iota(jnp.int32, (ALL, ALL), 1).astype(F32)
    earlier = (row_b < row_a) & (floor_div(row_a, 24) == floor_div(row_b, 24))
    before = dot(jnp.where(earlier, 1.0, 0.0).astype(BF), hit.astype(BF))
    mark = jnp.where(hit > 0, before + 1.0, 0.0).astype(BF)
    mix_a = mix.astype(BF)
    mix_b = (mix - mix_a.astype(F32)).astype(BF)

    slot = lax.broadcasted_iota(jnp.int32, (SLOTS, 64), 0).astype(F32)
    z, ex, _, _ = slot_fields(slot)
    e_here = lax.broadcasted_iota(jnp.int32, (SLOTS, 64), 1).astype(F32)
    pick = jnp.where(e_here == 8 * z + 2 * x_here + ex, 1.0, 0.0).astype(BF)
    marked = dot(pick, mark, ((1,), (1,)))
    slot = lax.broadcasted_iota(jnp.int32, (SLOTS, ALL), 0).astype(F32)
    _, _, block, spot = slot_fields(slot)
    row = lax.broadcasted_iota(jnp.int32, (SLOTS, ALL), 1).astype(F32)
    chosen = (marked == spot + 1.0) & (floor_div(row, 24) == block)
    send[...] = jnp.where(chosen, 1.0, 0.0).astype(BF)

    slot = lax.broadcasted_iota(jnp.int32, (64, SLOTS), 1).astype(F32)
    z, ex, _, _ = slot_fields(slot)
    e_here = lax.broadcasted_iota(jnp.int32, (64, SLOTS), 0).astype(F32)
    pick = jnp.where(e_here == 8 * z + 2 * x_here + ex, 1.0, 0.0).astype(BF)
    marked = dot(mark, pick)
    slot = lax.broadcasted_iota(jnp.int32, (ALL, SLOTS), 1).astype(F32)
    _, _, block, spot = slot_fields(slot)
    row = lax.broadcasted_iota(jnp.int32, (ALL, SLOTS), 0).astype(F32)
    chosen = (marked == spot + 1.0) & (floor_div(row, 24) == block)
    mix_high[...] = jnp.where(chosen, dot(mix_a, pick), 0.0).astype(BF)
    mix_low[...] = jnp.where(chosen, dot(mix_b, pick), 0.0).astype(BF)


def routes(place, tables):
    vm = pl.BlockSpec(memory_space=pltpu.VMEM)
    return pl.pallas_call(
        routes_kernel,
        in_specs=[pl.BlockSpec(memory_space=pltpu.SMEM)] + [vm] * 4,
        out_specs=[vm] * 3,
        out_shape=[
            jax.ShapeDtypeStruct((SLOTS, ALL), BF),
            jax.ShapeDtypeStruct((ALL, SLOTS), BF),
            jax.ShapeDtypeStruct((ALL, SLOTS), BF),
        ],
        scratch_shapes=[pltpu.VMEM((ALL, TOPK), F32), pltpu.VMEM((ALL, TOPK), F32)],
        compiler_params=params(),
        name="routes",
    )(place, *tables)


def dispatch_kernel(place, h0, h1, h2, h3, p0, p1, p2, p3, send, packed, mine, rows):
    for d, (h, p) in enumerate(zip((h0, h1, h2, h3), (p0, p1, p2, p3))):
        there = lax.rem(place[1] + d, NX)
        at = pl.multiple_of(there * ROWS, 16)
        rows[pl.ds(at, ROWS), :] = h[...].astype(F32)
    for d, p in enumerate((p0, p1, p2, p3)):
        at = pl.multiple_of(lax.rem(place[1] + d, NX) * HEAD, HEAD)
        rows[:, pl.ds(at, HEAD)] = rows[:, pl.ds(at, HEAD)] + p[...].astype(F32)
    mine[...] = rows[pl.ds(pl.multiple_of(place[1] * ROWS, 16), ROWS), :]
    packed[...] = dot(send[...], rows[...].astype(BF)).astype(BF)


def dispatch(place, hidden, projected, send):
    vm = pl.BlockSpec(memory_space=pltpu.VMEM)
    return pl.pallas_call(
        dispatch_kernel,
        in_specs=[pl.BlockSpec(memory_space=pltpu.SMEM)] + [vm] * 9,
        out_specs=[vm] * 2,
        out_shape=[
            jax.ShapeDtypeStruct((SLOTS, COLS), BF),
            jax.ShapeDtypeStruct((ROWS, COLS), F32),
        ],
        scratch_shapes=[pltpu.VMEM((ALL, COLS), F32)],
        compiler_params=params(),
        name="dispatch",
    )(place, *hidden, *projected, send)


AROUND = [(0, 0), (0, 1), (1, 0), (1, 1), (3, 0), (3, 1), (2, 0), (2, 1)]


def up_kernel(around, first, last, place, *refs):
    count = len(around)
    xs, gates, ups = refs[:count], refs[count : 2 * count], refs[2 * count : 3 * count]
    refs = refs[3 * count :]
    if first:
        both = jnp.zeros((2 * FFS, EXPERT_ROWS), F32)
        square = jnp.zeros((EXPERT_ROWS, HEAD), F32)
    else:
        both, square = refs[0][0], refs[1][0]
        refs = refs[2:]
    for x, wg, wu in zip(xs, gates, ups):
        rows = x[...].reshape(EXPERT_ROWS, COLS)
        weights = jnp.concatenate([wg[0], wu[0]], axis=0)
        both = both + dot(weights, rows, ((1,), (1,)))
        for m in range(COLS // HEAD):
            wide = rows[:, m * HEAD : (m + 1) * HEAD].astype(F32)
            square = square + wide * wide
    if last:
        total = lax.dot_general(
            jnp.ones((8, HEAD), F32),
            square,
            (((1,), (1,)), ((), ())),
            precision=lax.Precision.HIGHEST,
            preferred_element_type=F32,
        )[0:1]
        scale = lax.rsqrt(total * (1.0 / WIDTH) + EPS)
        v = both[0:FFS] * scale
        refs[0][...] = (v / (1.0 + jnp.exp(-v)) * (both[FFS:] * scale)).astype(BF)
    else:
        refs[0][0], refs[1][0] = both, square


def column_of(dy, dc):
    def index(e, place):
        core = place[3]
        return e, 0, lax.rem(place[2] + dy, NY) * NCORE + (1 - core if dc else core)

    return index


def expert_up(place, around, xs, wg, wu, sums=()):
    last = len(sums) > 0
    w_specs = [pl.BlockSpec((1, FFS, COLS), column_of(dy, dc)) for dy, dc in around]
    shapes = [(2, 2 * FFS, EXPERT_ROWS), (2, EXPERT_ROWS, HEAD)]
    sum_specs = [pl.BlockSpec((1,) + shape[1:], lambda e, p: (e, 0, 0)) for shape in shapes]
    x_specs = []
    for x in xs:
        if x.shape[1] == 2:
            x_specs.append(pl.BlockSpec((NZ, 1, ROWS, COLS), lambda e, p: (0, e, 0, 0)))
        else:
            x_specs.append(pl.BlockSpec((1, EXPERT_ROWS, COLS), lambda e, p: (e, 0, 0)))
    if last:
        out_specs = pl.BlockSpec((FFS, EXPERT_ROWS), lambda e, p: (e, 0))
        out_shape = jax.ShapeDtypeStruct((2 * FFS, EXPERT_ROWS), BF)
    else:
        out_specs = sum_specs
        out_shape = [jax.ShapeDtypeStruct(shape, F32) for shape in shapes]
    n = len(xs)
    return pl.pallas_call(
        functools.partial(up_kernel, around, not last, last),
        grid_spec=pltpu.PrefetchScalarGridSpec(
            num_scalar_prefetch=1,
            grid=(2,),
            in_specs=x_specs + w_specs + w_specs + (sum_specs if last else []),
            out_specs=out_specs,
        ),
        out_shape=out_shape,
        compiler_params=params(50),
        cost_estimate=pl.CostEstimate(
            flops=n * 1000000000, bytes_accessed=n * 2000000, transcendentals=0
        ),
        name="expert_up",
    )(place, *xs, *[wg] * n, *[wu] * n, *sums)


def split_kernel(place, w, *outs):
    for out, (dy, dc) in zip(outs, AROUND):
        core = place[3]
        there = lax.rem(place[2] + NY - dy, NY) * NCORE + (1 - core if dc else core)
        out[...] = w[:, :, pl.ds(pl.multiple_of(there * COLS, COLS), COLS)]


def split_down(place, w):
    return pl.pallas_call(
        split_kernel,
        grid=(2,),
        in_specs=[
            pl.BlockSpec(memory_space=pltpu.SMEM),
            pl.BlockSpec((1, FFS, WIDTH), lambda e: (e, 0, 0)),
        ],
        out_specs=[pl.BlockSpec((1, FFS, COLS), lambda e: (e, 0, 0))] * NC,
        out_shape=[jax.ShapeDtypeStruct((2, FFS, COLS), BF)] * NC,
        compiler_params=params(62),
        name="split_down",
    )(place, w)


def down_kernel(count, last, *refs):
    hs, ws, refs = refs[:count], refs[count : 2 * count], refs[2 * count :]
    total = dot(hs[0][...], ws[0][0], ((0,), (0,)))
    for h, w in zip(hs[1:], ws[1:]):
        total = total + dot(h[...], w[0], ((0,), (0,)))
    if last:
        total = total + refs[0][0]
        refs[1][...] = total.astype(BF).reshape(NZ, 1, ROWS, COLS)
    else:
        refs[0][0] = total


def expert_down(hs, ws, total=None):
    n, last = len(hs), total is not None
    sum_spec = pl.BlockSpec((1, EXPERT_ROWS, COLS), lambda e: (e, 0, 0))
    if last:
        out_spec = pl.BlockSpec((NZ, 1, ROWS, COLS), lambda e: (0, e, 0, 0))
        out_shape = jax.ShapeDtypeStruct((NZ, 2, ROWS, COLS), BF)
    else:
        out_spec, out_shape = sum_spec, jax.ShapeDtypeStruct((2, EXPERT_ROWS, COLS), F32)
    return pl.pallas_call(
        functools.partial(down_kernel, n, last),
        grid=(2,),
        in_specs=[pl.BlockSpec((FFS, EXPERT_ROWS), lambda e: (e, 0))] * n
        + [pl.BlockSpec((1, FFS, COLS), lambda e: (e, 0, 0))] * n
        + ([sum_spec] if last else []),
        out_specs=out_spec,
        out_shape=out_shape,
        compiler_params=params(62),
        cost_estimate=pl.CostEstimate(
            flops=n * 700000000, bytes_accessed=n * 1000000, transcendentals=0
        ),
        name="expert_down",
    )(*hs, *ws, *([total] if last else []))


def mix_kernel(place, back, mix_high, mix_low, o0, o1, o2, o3, rows):
    rows[...] = dot(mix_high[...], back[...]) + dot(mix_low[...], back[...])
    for d, o in enumerate((o0, o1, o2, o3)):
        at = pl.multiple_of(lax.rem(place[1] + d, NX) * ROWS, 16)
        o[...] = rows[pl.ds(at, ROWS), :].astype(o.dtype)


def mix_back(place, back, mix_high, mix_low):
    vm = pl.BlockSpec(memory_space=pltpu.VMEM)
    return pl.pallas_call(
        mix_kernel,
        in_specs=[pl.BlockSpec(memory_space=pltpu.SMEM)] + [vm] * 3,
        out_specs=[vm] * 4,
        out_shape=[jax.ShapeDtypeStruct((ROWS, COLS), F32)]
        + [jax.ShapeDtypeStruct((ROWS, COLS), BF)] * 3,
        scratch_shapes=[pltpu.VMEM((ALL, COLS), F32)],
        compiler_params=params(),
        name="mix_back",
    )(place, back, mix_high, mix_low)


def from_x(value, d):
    return lax.ppermute(value, "x", [((i + d) % NX, i) for i in range(NX)])


def in_rows(value):
    return value.transpose(0, 2, 1, 3).reshape(ROWS, value.shape[3])


def along_x(value):
    return [value] + [from_x(value, d) for d in range(1, NX)]


def from_y(value, d):
    return lax.ppermute(value, "y", [((i + d) % NY, i) for i in range(NY)])


def other_core(value):
    return lax.ppermute(value, "core", [(0, 1), (1, 0)])


def from_ctx(value, dy, dc):
    pairs = []
    for y in range(NY):
        for core in range(NCORE):
            source = (y + dy) % NY * NCORE + (core ^ dc)
            pairs.append((source, y * NCORE + core))
    return lax.ppermute(value, CTX, pairs)


def body(
    kv_cache,
    slot_owner,
    slot_fill,
    phased,
    phase_owner,
    phase_fill,
    relay_page,
    relay_slot,
    queries,
    new_kv,
    hidden_in,
    o_proj,
    expert_ids,
    gate_weights,
    w_gate,
    w_up,
    w_down,
):
    del relay_slot
    ctx = lax.axis_index(CTX)
    place = [ctx, lax.axis_index("x"), lax.axis_index("y"), lax.axis_index("core")]
    place = jnp.stack(place).astype(jnp.int32)

    with jax.named_scope("gather_projection"):
        o_cols = lax.all_gather(o_proj, "z")
    with jax.named_scope("attend"):
        parts = attention(
            place,
            slot_owner,
            slot_fill,
            phase_owner,
            phase_fill,
            relay_page[0],
            queries.transpose(0, 2, 1, 3),
            kv_cache[0],
            phased[0],
            new_kv.reshape(ROWS, 2 * KV_HEADS * HEAD),
        )
    with jax.named_scope("gather_tables"):
        parts, expert_ids, gate_weights, hidden_in, w_down = lax.optimization_barrier(
            (parts, expert_ids, gate_weights, hidden_in, w_down)
        )
        hidden = along_x(in_rows(lax.dynamic_slice_in_dim(hidden_in, ctx * COLS, COLS, 3)))
        tables = along_x(jnp.stack([in_rows(expert_ids).astype(F32), in_rows(gate_weights)]))
        down_parts = split_down(place, w_down)
    with jax.named_scope("join_parts"):
        parts = lax.all_to_all(parts, CTX, 0, 0, tiled=True)
        parts, tables, hidden, down_parts = lax.optimization_barrier(
            (parts, tables, hidden, down_parts)
        )
        attended = join(parts)
    with jax.named_scope("turn_down"):
        down_cols = list(down_parts)
        for n in (6, 7):
            down_cols[n] = from_ctx(down_parts[n], *AROUND[n])
    with jax.named_scope("project_rows"):
        partial = project(place, along_x(attended), o_cols)
    with jax.named_scope("sum_projection"):
        columns = lax.all_to_all(partial, CTX, 0, 0, tiled=True)
        columns, down_cols = lax.optimization_barrier((columns, down_cols))
        projected = along_x(add_up(columns))
    with jax.named_scope("turn_down"):
        for n in range(1, 6):
            down_cols[n] = from_ctx(down_cols[n], *AROUND[n])
    with jax.named_scope("find_routes"):
        send, mix_high, mix_low = routes(place, tables)
    with jax.named_scope("dispatch_rows"):
        packed, mine = dispatch(place, hidden, projected, send)
        arrived = lax.all_to_all(packed.reshape(NZ, 96, COLS), "z", 0, 0, tiled=True)
        arrived = arrived.reshape(NZ, 2, ROWS, COLS)
        arrived, down_cols = lax.optimization_barrier((arrived, down_cols))
    with jax.named_scope("gather_rows"):
        after, before = from_y(arrived, 1), from_y(arrived, 3)
        far = [from_y(after[:, 0], 1), from_y(before[:, 1], 3)]
        near = []
        for value in (arrived, after, before):
            near += [value, other_core(value)]
    with jax.named_scope("up"):
        gate_t, up_t = w_gate.transpose(0, 2, 1), w_up.transpose(0, 2, 1)
        sums = expert_up(place, AROUND[:6], near, gate_t, up_t)
        sums, far = lax.optimization_barrier((sums, far))
        far = jnp.stack(far).reshape(2, EXPERT_ROWS, COLS)
        units = expert_up(place, AROUND[6:], [far, other_core(far)], gate_t, up_t, sums)
    with jax.named_scope("gather_units"):
        after, before, far = from_y(units, 1), from_y(units, 3), from_y(units, 2)
        near = []
        for value in (units, after, before):
            near += [value, other_core(value)]
    with jax.named_scope("down"):
        total = expert_down(near, down_cols[:6])
        total, far = lax.optimization_barrier((total, far))
        outcome = expert_down([far, other_core(far)], down_cols[6:], total)
    with jax.named_scope("return_rows"):
        back = lax.all_to_all(outcome.reshape(NZ, 96, COLS), "z", 0, 0, tiled=True)
    with jax.named_scope("mix"):
        mixed = mix_back(place, back.reshape(SLOTS, COLS), mix_high, mix_low)
        total = mine + mixed[0]
        for d in range(1, NX):
            total = total + from_x(mixed[d], NX - d).astype(F32)
    return total.astype(BF).reshape(2, 6, 4, COLS).transpose(0, 2, 1, 3)


def solution(mesh):
    inner = Mesh(mesh.devices.reshape(NY, NCORE, NZ, NX), ("y", "core", "z", "x"))
    exp = ("z", "x")
    in_specs = (
        P(exp, CTX, None, None, None),
        P(exp, CTX),
        P(exp, CTX),
        P(exp, CTX, None, None, None),
        P(exp, None),
        P(exp, None),
        P(exp, None, None),
        P(exp, None, None),
        P(None, exp, None, None),
        P(None, exp, None, None, None),
        P(None, exp, None, None),
        P(CTX, exp),
        P(None, exp, None, None),
        P(None, exp, None, None),
        P(exp, None, CTX),
        P(exp, None, CTX),
        P(exp, CTX, None),
    )
    out_specs = P(None, exp, None, CTX)
    return jax.shard_map(body, mesh=inner, in_specs=in_specs, out_specs=out_specs, check_vma=False)
```

```python
import functools

import jax
import jax.numpy as jnp
from jax import lax
from jax.experimental import pallas as pl
from jax.experimental.pallas import tpu as pltpu
from jax.sharding import Mesh, PartitionSpec as P

HEADS = 64
KV_HEADS = 4
HEAD = 128
TOPK = 8
NY, NCORE, NZ, NX = 4, 2, 8, 4
NC = NY * NCORE
ROWS = 48
ALL = NX * ROWS
KEYS = 1152
CAP = 6
EXPERT_ROWS = 384
SLOTS = NZ * 2 * NX * 2 * CAP
WIDTH = 4096
COLS = WIDTH // NC
FFS = 192
SCALE = HEAD ** (-0.5)
EPS = 1e-06
UP_MB = 24
MASKED = -1e30
CTX = ("y", "core")
BF = jnp.bfloat16
F32 = jnp.float32


def params(mb=16):
    return pltpu.CompilerParams(vmem_limit_bytes=mb * 1024 * 1024)


def dot(a, b, dims=((1,), (0,))):
    return lax.dot_general(a, b, (dims, ((), ())), preferred_element_type=F32)


def thresholds(value, step, count):
    total = jnp.zeros_like(value)
    for n in range(1, count):
        total = total + (value >= n * step).astype(value.dtype)
    return total


def attention_kernel(
    place, owner, fill, phase_owner, phase_fill, relay, q, kv, ph, fk, fv, out, bias, keys, vals, qf, fresh_k, fresh_v
):
    @pl.when(pl.program_id(0) == 0)
    def _():
        me = place[0]
        key = lax.broadcasted_iota(jnp.int32, (8, KEYS), 1)
        page = lax.shift_right_logical(key, 5)
        own = jnp.full((8, KEYS), -1, jnp.int32)
        cap = jnp.zeros((8, KEYS), jnp.int32)
        for p in range(24):
            own = jnp.where(page == p, owner[0, p], own)
            cap = jnp.where(page == p, fill[0, p], cap)
        for p in range(8):
            sent = relay[me, 0] == p
            for d in range(1, NC):
                sent = sent | (relay[me, d] == p)
            at = me * 8 + p
            own = jnp.where(page == 24 + p, jnp.where(sent, phase_owner[0, at], -1), own)
            cap = jnp.where(page == 24 + p, phase_fill[0, at], cap)
        own = jnp.where((key & 31) < cap, own, -1)[0:1]
        row = lax.broadcasted_iota(jnp.int32, (ROWS, KEYS), 0)
        step = thresholds(row, 24, 2)
        rest = row - 24 * step
        draft = lax.shift_right_logical(rest, 2)
        req = rest & 3
        fresh = lax.broadcasted_iota(jnp.int32, (ROWS, KEYS), 1) - 1024
        f_step = thresholds(fresh, 24, 2)
        f_rest = fresh - 24 * f_step
        f_req = thresholds(f_rest, 6, 4)
        f_draft = f_rest - 6 * f_req
        earlier = (f_step < step) | ((f_step == step) & (f_draft <= draft))
        is_fresh = (fresh >= 0) & (fresh < ROWS) & (f_req == req) & earlier
        is_fresh = is_fresh & (jnp.full((ROWS, KEYS), me, jnp.int32) == 0)
        seen = (jnp.broadcast_to(own, (ROWS, KEYS)) == req) | is_fresh
        bias[...] = jnp.where(seen, 0.0, MASKED)
        keys[1024 + ROWS :, :] = jnp.zeros((KEYS - 1024 - ROWS, HEAD), BF)
        vals[1024 + ROWS :, :] = jnp.zeros((KEYS - 1024 - ROWS, HEAD), BF)

    keys[0:768, :] = kv[:, 0].reshape(768, HEAD)
    keys[768:1024, :] = ph[:, 0].reshape(256, HEAD)
    vals[0:768, :] = kv[:, 1].reshape(768, HEAD)
    vals[768:1024, :] = ph[:, 1].reshape(256, HEAD)
    for n in range(ROWS):
        at = (n // 24, n % 24 // 6, n % 6)
        fresh_k[2 * n : 2 * n + 2, :] = fk[at].astype(F32)
        fresh_v[2 * n : 2 * n + 2, :] = fv[at].astype(F32)
    keys[1024 : 1024 + ROWS, :] = fresh_k[pl.ds(0, ROWS, 2), :].astype(BF)
    vals[1024 : 1024 + ROWS, :] = fresh_v[pl.ds(1, ROWS, 2), :].astype(BF)
    for n in range(12):
        qf[n * 4 : n * 4 + 4, :] = q[n // 6, n % 6].astype(F32)
    lane = lax.broadcasted_iota(jnp.int32, (ROWS, HEAD), 1)
    for half in range(2):
        ext = jnp.zeros((ROWS, HEAD), F32)
        for h0 in range(0, 8, 4):
            parts = []
            for h in range(h0, h0 + 4):
                g = half * 8 + h
                parts.append(qf[:, g * HEAD : (g + 1) * HEAD].astype(BF))
            qs = jnp.concatenate(parts, axis=0)
            s = dot(qs, keys[...], ((1,), (1,)))
            s = (s.reshape(4, ROWS, KEYS) + bias[...][None]).reshape(4 * ROWS, KEYS)
            top = jnp.max(s, axis=-1, keepdims=True)
            p = jnp.exp((s - top) * SCALE)
            mass = jnp.sum(p, axis=-1, keepdims=True)
            o = dot(p.astype(BF), vals[...]) / mass
            for n in range(4):
                h = h0 + n
                rows = slice(n * ROWS, (n + 1) * ROWS)
                out[half, :, h * HEAD : (h + 1) * HEAD] = o[rows].astype(BF)
                ext = jnp.where(lane == h, top[rows], ext)
                ext = jnp.where(lane == 64 + h, mass[rows], ext)
        high = ext.astype(BF).astype(F32)
        rest = ext - high
        mid = rest.astype(BF).astype(F32)
        low = rest - mid
        packed = high + pltpu.roll(mid, 8, 1) + pltpu.roll(low, 16, 1)
        out[half, :, 8 * HEAD : 9 * HEAD] = packed.astype(BF)


def attention(place, owner, fill, phase_owner, phase_fill, relay, q, kv, ph, fresh):
    smem = pl.BlockSpec(memory_space=pltpu.SMEM)
    return pl.pallas_call(
        attention_kernel,
        grid=(KV_HEADS,),
        in_specs=[smem] * 6
        + [
            pl.BlockSpec((2, 6, 4, 16 * HEAD), lambda k: (0, 0, 0, k)),
            pl.BlockSpec((24, 2, 32, HEAD), lambda k: (0, 0, 0, k)),
            pl.BlockSpec((8, 2, 32, HEAD), lambda k: (0, 0, 0, k)),
            pl.BlockSpec((2, 4, 6, 2, HEAD), lambda k: (0, 0, 0, 0, k)),
            pl.BlockSpec((2, 4, 6, 2, HEAD), lambda k: (0, 0, 0, 0, k)),
        ],
        out_specs=pl.BlockSpec((2, ROWS, 9 * HEAD), lambda k: (k, 0, 0)),
        out_shape=jax.ShapeDtypeStruct((NC, ROWS, 9 * HEAD), BF),
        scratch_shapes=[
            pltpu.VMEM((ROWS, KEYS), F32),
            pltpu.VMEM((KEYS, HEAD), BF),
            pltpu.VMEM((KEYS, HEAD), BF),
            pltpu.VMEM((ROWS, 16 * HEAD), F32),
            pltpu.VMEM((2 * ROWS, HEAD), F32),
            pltpu.VMEM((2 * ROWS, HEAD), F32),
        ],
        compiler_params=params(62),
        name="attention",
    )(place, owner, fill, phase_owner, phase_fill, relay, q, kv, ph, fresh, fresh)


def join_kernel(parts, out):
    tops, masses = [], []
    for c in range(NC):
        ext = parts[c, :, 8 * HEAD :].astype(F32)
        ext = ext + pltpu.roll(ext, HEAD - 8, 1) + pltpu.roll(ext, HEAD - 16, 1)
        tops.append(ext)
        masses.append(pltpu.roll(ext, 64, 1))
    best = functools.reduce(jnp.maximum, tops)
    weights = [m * jnp.exp((t - best) * SCALE) for t, m in zip(tops, masses)]
    total = functools.reduce(jnp.add, weights)
    shares = [w / total for w in weights]
    for h in range(8):
        cols = slice(h * HEAD, (h + 1) * HEAD)
        acc = shares[0][:, h : h + 1] * parts[0, :, cols].astype(F32)
        for c in range(1, NC):
            acc = acc + shares[c][:, h : h + 1] * parts[c, :, cols].astype(F32)
        out[:, cols] = acc.astype(BF)


def join(parts):
    return pl.pallas_call(
        join_kernel,
        out_shape=jax.ShapeDtypeStruct((ROWS, 8 * HEAD), BF),
        compiler_params=params(),
        name="join",
    )(parts)


def project_kernel(place, a0, a1, a2, a3, w, out, rows):
    @pl.when(pl.program_id(0) == 0)
    def _():
        for d, a in enumerate((a0, a1, a2, a3)):
            at = pl.multiple_of(lax.rem(place[1] + d, NX) * ROWS, 16)
            rows[pl.ds(at, ROWS), :] = a[...]

    for n in range(0, NZ // 2, 2):
        both = dot(rows[...], jnp.concatenate([w[n], w[n + 1]], axis=1)).astype(BF)
        out[n], out[n + 1] = both[:, 0:HEAD], both[:, HEAD:]


def project(place, pieces, w):
    whole = pl.BlockSpec((ROWS, 8 * HEAD), lambda k: (0, 0))
    return pl.pallas_call(
        project_kernel,
        grid=(2,),
        in_specs=[pl.BlockSpec(memory_space=pltpu.SMEM)]
        + [whole] * 4
        + [pl.BlockSpec((NZ // 2, 8 * HEAD, HEAD), lambda k: (k, 0, 0))],
        out_specs=pl.BlockSpec((NZ // 2, ALL, HEAD), lambda k: (k, 0, 0)),
        out_shape=jax.ShapeDtypeStruct((NZ, ALL, HEAD), BF),
        scratch_shapes=[pltpu.VMEM((ALL, 8 * HEAD), BF)],
        compiler_params=params(62),
        name="project",
    )(place, *pieces, w)


def add_kernel(parts, out):
    acc = parts[0].astype(F32)
    for c in range(1, NC):
        acc = acc + parts[c].astype(F32)
    out[...] = acc.astype(BF)


def add_up(parts):
    return pl.pallas_call(
        add_kernel,
        out_shape=jax.ShapeDtypeStruct((ALL, HEAD), BF),
        compiler_params=params(),
        name="add_up",
    )(parts)


def floor_div(value, by):
    return jnp.floor((value + 0.5) * (1.0 / by))


def slot_fields(value):
    z = floor_div(value, 96)
    rest = value - 96 * z
    ex = floor_div(rest, 48)
    rest = rest - 48 * ex
    block = floor_div(rest, CAP)
    spot = rest - CAP * block
    return z, ex, block, spot


def routes_kernel(place, t0, t1, t2, t3, send, mix_high, mix_low, ids, gates):
    for d, t in enumerate((t0, t1, t2, t3)):
        at = pl.multiple_of(lax.rem(place[1] + d, NX) * ROWS, 16)
        ids[pl.ds(at, ROWS), :] = t[0]
        gates[pl.ds(at, ROWS), :] = t[1]
    x_here = place[1].astype(F32)
    expert = lax.broadcasted_iota(jnp.int32, (ALL, 64), 1).astype(F32)
    gate_rows = gates[...]
    share = gate_rows / jnp.sum(gate_rows, axis=-1, keepdims=True)
    id_rows = ids[...]
    hit = jnp.zeros((ALL, 64), F32)
    mix = jnp.zeros((ALL, 64), F32)
    for k in range(TOPK):
        same = id_rows[:, k : k + 1] == expert
        hit = jnp.where(same, 1.0, hit)
        mix = jnp.where(same, share[:, k : k + 1], mix)
    row_a = lax.broadcasted_iota(jnp.int32, (ALL, ALL), 0).astype(F32)
    row_b = lax.broadcasted_iota(jnp.int32, (ALL, ALL), 1).astype(F32)
    earlier = (row_b < row_a) & (floor_div(row_a, 24) == floor_div(row_b, 24))
    before = dot(jnp.where(earlier, 1.0, 0.0).astype(BF), hit.astype(BF))
    mark = jnp.where(hit > 0, before + 1.0, 0.0).astype(BF)
    mix_a = mix.astype(BF)
    mix_b = (mix - mix_a.astype(F32)).astype(BF)

    slot = lax.broadcasted_iota(jnp.int32, (SLOTS, 64), 0).astype(F32)
    z, ex, _, _ = slot_fields(slot)
    e_here = lax.broadcasted_iota(jnp.int32, (SLOTS, 64), 1).astype(F32)
    pick = jnp.where(e_here == 8 * z + 2 * x_here + ex, 1.0, 0.0).astype(BF)
    marked = dot(pick, mark, ((1,), (1,)))
    slot = lax.broadcasted_iota(jnp.int32, (SLOTS, ALL), 0).astype(F32)
    _, _, block, spot = slot_fields(slot)
    row = lax.broadcasted_iota(jnp.int32, (SLOTS, ALL), 1).astype(F32)
    chosen = (marked == spot + 1.0) & (floor_div(row, 24) == block)
    send[...] = jnp.where(chosen, 1.0, 0.0).astype(BF)

    slot = lax.broadcasted_iota(jnp.int32, (64, SLOTS), 1).astype(F32)
    z, ex, _, _ = slot_fields(slot)
    e_here = lax.broadcasted_iota(jnp.int32, (64, SLOTS), 0).astype(F32)
    pick = jnp.where(e_here == 8 * z + 2 * x_here + ex, 1.0, 0.0).astype(BF)
    marked = dot(mark, pick)
    slot = lax.broadcasted_iota(jnp.int32, (ALL, SLOTS), 1).astype(F32)
    _, _, block, spot = slot_fields(slot)
    row = lax.broadcasted_iota(jnp.int32, (ALL, SLOTS), 0).astype(F32)
    chosen = (marked == spot + 1.0) & (floor_div(row, 24) == block)
    mix_high[...] = jnp.where(chosen, dot(mix_a, pick), 0.0).astype(BF)
    mix_low[...] = jnp.where(chosen, dot(mix_b, pick), 0.0).astype(BF)


def routes(place, tables):
    vm = pl.BlockSpec(memory_space=pltpu.VMEM)
    return pl.pallas_call(
        routes_kernel,
        in_specs=[pl.BlockSpec(memory_space=pltpu.SMEM)] + [vm] * 4,
        out_specs=[vm] * 3,
        out_shape=[
            jax.ShapeDtypeStruct((SLOTS, ALL), BF),
            jax.ShapeDtypeStruct((ALL, SLOTS), BF),
            jax.ShapeDtypeStruct((ALL, SLOTS), BF),
        ],
        scratch_shapes=[pltpu.VMEM((ALL, TOPK), F32), pltpu.VMEM((ALL, TOPK), F32)],
        compiler_params=params(),
        name="routes",
    )(place, *tables)


def dispatch_kernel(place, h0, h1, h2, h3, p0, p1, p2, p3, send, packed, mine, rows):
    for d, (h, p) in enumerate(zip((h0, h1, h2, h3), (p0, p1, p2, p3))):
        there = lax.rem(place[1] + d, NX)
        at = pl.multiple_of(there * ROWS, 16)
        rows[pl.ds(at, ROWS), :] = h[...].astype(F32)
    for d, p in enumerate((p0, p1, p2, p3)):
        at = pl.multiple_of(lax.rem(place[1] + d, NX) * HEAD, HEAD)
        rows[:, pl.ds(at, HEAD)] = rows[:, pl.ds(at, HEAD)] + p[...].astype(F32)
    mine[...] = rows[pl.ds(pl.multiple_of(place[1] * ROWS, 16), ROWS), :]
    packed[...] = dot(send[...], rows[...].astype(BF)).astype(BF)


def dispatch(place, hidden, projected, send):
    vm = pl.BlockSpec(memory_space=pltpu.VMEM)
    return pl.pallas_call(
        dispatch_kernel,
        in_specs=[pl.BlockSpec(memory_space=pltpu.SMEM)] + [vm] * 9,
        out_specs=[vm] * 2,
        out_shape=[
            jax.ShapeDtypeStruct((SLOTS, COLS), BF),
            jax.ShapeDtypeStruct((ROWS, COLS), F32),
        ],
        scratch_shapes=[pltpu.VMEM((ALL, COLS), F32)],
        compiler_params=params(),
        name="dispatch",
    )(place, *hidden, *projected, send)


AROUND = [(0, 0), (0, 1), (1, 0), (1, 1), (3, 0), (3, 1), (2, 0), (2, 1)]


def squares(rows):
    total = jnp.zeros((EXPERT_ROWS, HEAD), F32)
    for m in range(COLS // HEAD):
        wide = rows[:, m * HEAD : (m + 1) * HEAD].astype(F32)
        total = total + wide * wide
    return total


def up_near_kernel(place, *refs):
    n = 6
    xs, gates, ups, (both_out, square_out) = refs[:n], refs[n : 2 * n], refs[2 * n : 3 * n], refs[3 * n :]
    both = jnp.zeros((2 * FFS, EXPERT_ROWS), F32)
    square = jnp.zeros((EXPERT_ROWS, HEAD), F32)
    for x, wg, wu in zip(xs, gates, ups):
        rows = x[...].reshape(EXPERT_ROWS, COLS)
        both = both + dot(jnp.concatenate([wg[0], wu[0]], axis=0), rows, ((1,), (1,)))
        square = square + squares(rows)
    both_out[0], square_out[0] = both, square


def up_far_kernel(place, *refs):
    xs, gates, ups, (both_in, square_in, out) = refs[:4], refs[4:6], refs[6:8], refs[8:]
    for e in range(2):
        both, square = both_in[e], square_in[e]
        for x, wg, wu in zip(xs[2 * e : 2 * e + 2], gates, ups):
            rows = x[...].reshape(EXPERT_ROWS, COLS)
            both = both + dot(jnp.concatenate([wg[e], wu[e]], axis=0), rows, ((1,), (1,)))
            square = square + squares(rows)
        total = lax.dot_general(
            jnp.ones((8, HEAD), F32),
            square,
            (((1,), (1,)), ((), ())),
            precision=lax.Precision.HIGHEST,
            preferred_element_type=F32,
        )[0:1]
        scale = lax.rsqrt(total * (1.0 / WIDTH) + EPS)
        v = both[0:FFS] * scale
        unit = (v / (1.0 + jnp.exp(-v)) * (both[FFS:] * scale)).astype(BF)
        out[e * FFS : (e + 1) * FFS, :] = unit


def columns_at(place, dy, dc):
    return lax.rem(place[2] + dy, NY) * NCORE + (1 - place[3] if dc else place[3])


SUMS = [(2, 2 * FFS, EXPERT_ROWS), (2, EXPERT_ROWS, HEAD)]


def expert_up_near(place, xs, wg, wu):
    def weight(dy, dc):
        return pl.BlockSpec((1, FFS, COLS), lambda e, p: (e, 0, columns_at(p, dy, dc)))

    weights = [weight(*at) for at in AROUND[:6]]
    return pl.pallas_call(
        up_near_kernel,
        grid_spec=pltpu.PrefetchScalarGridSpec(
            num_scalar_prefetch=1,
            grid=(2,),
            in_specs=[pl.BlockSpec((NZ, 1, ROWS, COLS), lambda e, p: (0, e, 0, 0))] * 6 + weights * 2,
            out_specs=[pl.BlockSpec((1,) + shape[1:], lambda e, p: (e, 0, 0)) for shape in SUMS],
        ),
        out_shape=[jax.ShapeDtypeStruct(shape, F32) for shape in SUMS],
        compiler_params=params(UP_MB),
        cost_estimate=pl.CostEstimate(flops=6000000000, bytes_accessed=12000000, transcendentals=0),
        name="expert_up",
    )(place, *xs, *[wg] * 6, *[wu] * 6)


def expert_up_far(place, xs, wg, wu, sums):
    def weight(dy, dc):
        return pl.BlockSpec((2, FFS, COLS), lambda i, p: (0, 0, columns_at(p, dy, dc)))

    whole = lambda shape: pl.BlockSpec(shape, lambda i, p: (0,) * len(shape))
    weights = [weight(*at) for at in AROUND[6:]]
    return pl.pallas_call(
        up_far_kernel,
        grid_spec=pltpu.PrefetchScalarGridSpec(
            num_scalar_prefetch=1,
            grid=(1,),
            in_specs=[whole((NZ, ROWS, COLS))] * 4 + weights * 2 + [whole(shape) for shape in SUMS],
            out_specs=whole((2 * FFS, EXPERT_ROWS)),
        ),
        out_shape=jax.ShapeDtypeStruct((2 * FFS, EXPERT_ROWS), BF),
        compiler_params=params(UP_MB),
        name="expert_up_far",
    )(place, *xs, wg, wg, wu, wu, *sums)


def split_kernel(place, w, *outs):
    for out, (dy, dc) in zip(outs, AROUND):
        core = place[3]
        there = lax.rem(place[2] + NY - dy, NY) * NCORE + (1 - core if dc else core)
        out[...] = w[:, :, pl.ds(pl.multiple_of(there * COLS, COLS), COLS)]


def split_down(place, w):
    return pl.pallas_call(
        split_kernel,
        grid=(2,),
        in_specs=[
            pl.BlockSpec(memory_space=pltpu.SMEM),
            pl.BlockSpec((1, FFS, WIDTH), lambda e: (e, 0, 0)),
        ],
        out_specs=[pl.BlockSpec((1, FFS, COLS), lambda e: (e, 0, 0))] * NC,
        out_shape=[jax.ShapeDtypeStruct((2, FFS, COLS), BF)] * NC,
        compiler_params=params(62),
        name="split_down",
    )(place, w)


def down_near_kernel(*refs):
    hs, ws, out = refs[:6], refs[6:12], refs[12]
    total = dot(hs[0][...], ws[0][0], ((0,), (0,)))
    for h, w in zip(hs[1:], ws[1:]):
        total = total + dot(h[...], w[0], ((0,), (0,)))
    out[0] = total


def expert_down_near(hs, ws):
    return pl.pallas_call(
        down_near_kernel,
        grid=(2,),
        in_specs=[pl.BlockSpec((FFS, EXPERT_ROWS), lambda e: (e, 0))] * 6
        + [pl.BlockSpec((1, FFS, COLS), lambda e: (e, 0, 0))] * 6,
        out_specs=pl.BlockSpec((1, EXPERT_ROWS, COLS), lambda e: (e, 0, 0)),
        out_shape=jax.ShapeDtypeStruct((2, EXPERT_ROWS, COLS), F32),
        compiler_params=params(),
        cost_estimate=pl.CostEstimate(flops=2000000000, bytes_accessed=6000000, transcendentals=0),
        name="expert_down",
    )(*hs, *ws)


def down_far_kernel(*refs):
    hs, ws, total_in, out = refs[:4], refs[4:6], refs[6], refs[7]
    for e in range(2):
        total = total_in[e]
        for h, w in zip(hs[2 * e : 2 * e + 2], ws):
            total = total + dot(h[...], w[e], ((0,), (0,)))
        out[:, e] = total.astype(BF).reshape(NZ, ROWS, COLS)


def expert_down_far(hs, ws, total):
    return pl.pallas_call(
        down_far_kernel,
        out_shape=jax.ShapeDtypeStruct((NZ, 2, ROWS, COLS), BF),
        compiler_params=params(),
        name="expert_down_far",
    )(*hs, *ws, total)


def mix_kernel(place, back, mix_high, mix_low, o0, o1, o2, o3, rows):
    rows[...] = dot(mix_high[...], back[...]) + dot(mix_low[...], back[...])
    for d, o in enumerate((o0, o1, o2, o3)):
        at = pl.multiple_of(lax.rem(place[1] + d, NX) * ROWS, 16)
        o[...] = rows[pl.ds(at, ROWS), :].astype(o.dtype)


def mix_back(place, back, mix_high, mix_low):
    vm = pl.BlockSpec(memory_space=pltpu.VMEM)
    return pl.pallas_call(
        mix_kernel,
        in_specs=[pl.BlockSpec(memory_space=pltpu.SMEM)] + [vm] * 3,
        out_specs=[vm] * 4,
        out_shape=[jax.ShapeDtypeStruct((ROWS, COLS), F32)]
        + [jax.ShapeDtypeStruct((ROWS, COLS), BF)] * 3,
        scratch_shapes=[pltpu.VMEM((ALL, COLS), F32)],
        compiler_params=params(),
        name="mix_back",
    )(place, back, mix_high, mix_low)


def from_x(value, d):
    return lax.ppermute(value, "x", [((i + d) % NX, i) for i in range(NX)])


def in_rows(value):
    return value.transpose(0, 2, 1, 3).reshape(ROWS, value.shape[3])


def along_x(value):
    return [value] + [from_x(value, d) for d in range(1, NX)]


def from_y(value, d):
    return lax.ppermute(value, "y", [((i + d) % NY, i) for i in range(NY)])


def other_core(value):
    return lax.ppermute(value, "core", [(0, 1), (1, 0)])


def from_ctx(value, dy, dc):
    pairs = []
    for y in range(NY):
        for core in range(NCORE):
            source = (y + dy) % NY * NCORE + (core ^ dc)
            pairs.append((source, y * NCORE + core))
    return lax.ppermute(value, CTX, pairs)


def body(
    kv_cache,
    slot_owner,
    slot_fill,
    phased,
    phase_owner,
    phase_fill,
    relay_page,
    relay_slot,
    queries,
    new_kv,
    hidden_in,
    o_proj,
    expert_ids,
    gate_weights,
    w_gate,
    w_up,
    w_down,
):
    del relay_slot
    ctx = lax.axis_index(CTX)
    place = [ctx, lax.axis_index("x"), lax.axis_index("y"), lax.axis_index("core")]
    place = jnp.stack(place).astype(jnp.int32)

    with jax.named_scope("gather_projection"):
        o_cols = lax.all_gather(o_proj, "z")
    with jax.named_scope("attend"):
        parts = attention(
            place,
            slot_owner,
            slot_fill,
            phase_owner,
            phase_fill,
            relay_page[0],
            queries.transpose(0, 2, 1, 3),
            kv_cache[0],
            phased[0],
            new_kv,
        )
    with jax.named_scope("gather_tables"):
        parts, expert_ids, gate_weights, hidden_in, w_down = lax.optimization_barrier(
            (parts, expert_ids, gate_weights, hidden_in, w_down)
        )
        hidden = along_x(in_rows(lax.dynamic_slice_in_dim(hidden_in, ctx * COLS, COLS, 3)))
        tables = along_x(jnp.stack([in_rows(expert_ids).astype(F32), in_rows(gate_weights)]))
        down_parts = split_down(place, w_down)
    with jax.named_scope("join_parts"):
        parts = lax.all_to_all(parts, CTX, 0, 0, tiled=True)
        parts, tables, hidden, down_parts = lax.optimization_barrier(
            (parts, tables, hidden, down_parts)
        )
        attended = join(parts)
    with jax.named_scope("turn_down"):
        down_cols = list(down_parts)
        down_cols[6] = from_ctx(down_parts[6], *AROUND[6])
    with jax.named_scope("project_rows"):
        partial = project(place, along_x(attended), o_cols)
    with jax.named_scope("sum_projection"):
        columns = lax.all_to_all(partial, CTX, 0, 0, tiled=True)
        columns, down_cols = lax.optimization_barrier((columns, down_cols))
        projected = along_x(add_up(columns))
    with jax.named_scope("turn_down"):
        for n in (1, 2, 4, 3, 5, 7):
            down_cols[n] = from_ctx(down_cols[n], *AROUND[n])
    with jax.named_scope("find_routes"):
        send, mix_high, mix_low = routes(place, tables)
    with jax.named_scope("dispatch_rows"):
        packed, mine = dispatch(place, hidden, projected, send)
        packed, down_cols[1], down_cols[2], down_cols[4] = lax.optimization_barrier(
            (packed, down_cols[1], down_cols[2], down_cols[4])
        )
        arrived = lax.all_to_all(packed.reshape(NZ, 96, COLS), "z", 0, 0, tiled=True)
        arrived = arrived.reshape(NZ, 2, ROWS, COLS)
        arrived, down_cols = lax.optimization_barrier((arrived, down_cols))
    with jax.named_scope("gather_rows"):
        after, before = from_y(arrived, 1), from_y(arrived, 3)
        far = [from_y(after[:, 0], 1), from_y(before[:, 1], 3)]
        near = []
        for value in (arrived, after, before):
            near += [value, other_core(value)]
    with jax.named_scope("up"):
        gate_t, up_t = w_gate.transpose(0, 2, 1), w_up.transpose(0, 2, 1)
        sums = expert_up_near(place, near, gate_t, up_t)
        sums, far = lax.optimization_barrier((sums, far))
        far = [far[0], other_core(far[0]), far[1], other_core(far[1])]
        units = expert_up_far(place, far, gate_t, up_t, sums)
    with jax.named_scope("gather_units"):
        after, before = from_y(units, 1), from_y(units, 3)
        far = [from_y(after[:FFS], 1), from_y(before[FFS:], 3)]
        near = []
        for value in (units, after, before):
            near += [value, other_core(value)]
    with jax.named_scope("down"):
        total = expert_down_near(near, down_cols[:6])
        total, far = lax.optimization_barrier((total, far))
        far = [far[0], other_core(far[0]), far[1], other_core(far[1])]
        outcome = expert_down_far(far, down_cols[6:], total)
    with jax.named_scope("return_rows"):
        back = lax.all_to_all(outcome.reshape(NZ, 96, COLS), "z", 0, 0, tiled=True)
    with jax.named_scope("mix"):
        mixed = mix_back(place, back.reshape(SLOTS, COLS), mix_high, mix_low)
        total = mine + mixed[0]
        for d in range(1, NX):
            total = total + from_x(mixed[d], NX - d).astype(F32)
    return total.astype(BF).reshape(2, 6, 4, COLS).transpose(0, 2, 1, 3)


def solution(mesh):
    inner = Mesh(mesh.devices.reshape(NY, NCORE, NZ, NX), ("y", "core", "z", "x"))
    exp = ("z", "x")
    in_specs = (
        P(exp, CTX, None, None, None),
        P(exp, CTX),
        P(exp, CTX),
        P(exp, CTX, None, None, None),
        P(exp, None),
        P(exp, None),
        P(exp, None, None),
        P(exp, None, None),
        P(None, exp, None, None),
        P(None, exp, None, None, None),
        P(None, exp, None, None),
        P(CTX, exp),
        P(None, exp, None, None),
        P(None, exp, None, None),
        P(exp, None, CTX),
        P(exp, None, CTX),
        P(exp, CTX, None),
    )
    out_specs = P(None, exp, None, CTX)
    return jax.shard_map(body, mesh=inner, in_specs=in_specs, out_specs=out_specs, check_vma=False)
```
